32 devices in a mesh: seq: 8 (over z, y), chan: 4 (over x, core).
Axes of the slice: x: 2, y: 2, z: 4, core: 2. Of those that a mesh axis runs over, the one named last changes fastest.
Arguments:
- tokens: bfloat16 [2048, 4096], P('seq', 'chan'), may hold values from -6 to 6
- w_in: bfloat16 [4096, 3, 4096], P(None, None, 'chan'), may hold values from -0.09375 to 0.09375
- short_filter: float32 [3, 3, 4096], P(None, None, 'chan'), may hold values from -3 to 3
- mr_filter: bfloat16 [256, 128], P('chan'), may hold values from -0.5 to 0.5
- skip_gain: float32 [4096], P('chan'), may hold values from -4 to 4
- w_out: bfloat16 [4096, 4096], P('chan'), may hold values from -0.09375 to 0.09375
- segments: int32 [2048], replicated, may hold values from 0 to 15, never falling along the last dimension, each value on 1 to 256 neighbouring positions
Outputs:
- mixed: bfloat16 [2048, 4096], P('seq', 'chan')
The draws below stay inside these ranges and needn't reach their ends.
Inputs may be any that keep to these rules, and one draw needn't show every extreme that they name: `segments`: document ids in contiguous sequence order never fall; each of the 16 documents holds 1 to 256 positions and one holds exactly that many.
All inputs are finite; a program needn't handle non-finite values.
Results may differ from the reference program's by a relative error of at most 0.0076.
Values may be sent and summed in bfloat16 or wider, within the bound.
A program may use at most 128 MiB of HBM per device.

```python
import math
import jax
import jax.numpy as jnp
import numpy as np
from jax import lax

D = 4096
GROUPS = 256
LEN = 128
SHORT = 3
DOCS = 16
TOKENS = 2048
GSIZE = 16
N_SEQ = 8


def steps_of(own_key, extent, cuts, smallest, high):
    loudness, own = 1.0, jax.random.fold_in(own_key, 6)
    for axis_at, shards_of in cuts:
        draws = jnp.exp(jax.random.uniform(jax.random.fold_in(own, axis_at), (shards_of,), jnp.float32, smallest / len(cuts), high / len(cuts)))
        loudness = loudness * jnp.repeat(draws, extent[axis_at] // shards_of).reshape([-1 if axis == axis_at else 1 for axis in range(len(extent))])
    return loudness


def profile(amount, total, bound, skew):
    loads = [(1 << 20) // math.isqrt(standing ** skew) + 1 for standing in range(2, amount + 1)]
    surplus, holding = total - bound - (amount - 1), [1] * (amount - 1)
    while surplus > 0:
        free = [i for i in range(amount - 1) if holding[i] < bound]
        whole, left = sum([loads[i] for i in free]), surplus
        for i in free:
            extra = min(bound - holding[i], max(1, left * loads[i] // whole), surplus)
            holding[i] = holding[i] + extra
            surplus = surplus - extra
    return np.array([bound] + holding)


def ragged(stream_key, count, total, bound, lean):
    if count == 2:
        one = jax.random.randint(stream_key, (), max(1, total - bound), min(bound, total - 1) + 1)
        return jnp.stack([one, total - one])
    lengths = jnp.asarray(profile(count, total, bound, lean), jnp.int32)
    pairs = (count - 1) // 2
    source_of, taker = lengths[1:1 + 2 * pairs:2], lengths[2:2 + 2 * pairs:2]
    slack = jnp.minimum(source_of - 1, bound - taker)
    passed = jax.random.randint(jax.random.fold_in(stream_key, 1), (pairs,), 0, 1 << 20) % (slack + 1)
    lengths = lengths.at[1:1 + 2 * pairs:2].set(source_of - passed).at[2:2 + 2 * pairs:2].set(taker + passed)
    return lengths[jax.random.permutation(jax.random.fold_in(stream_key, 2), count)]


def bell_draw(rng, dims, width, reach, shards=(), kind=jnp.bfloat16):
    result = jax.random.normal(rng, dims, jnp.float32) * width
    if len(shards) > 0:
        result = steps_of(rng, dims, shards, -0.22, 0.18) * result
    return jnp.clip(result, min=-reach, max=reach).astype(kind)


def setup_inputs(seed: int = 0) -> dict:
    streams_of = jax.random.split(jax.random.key(seed), 8)
    return {
        "tokens": bell_draw(streams_of[0], (TOKENS, D), 1.0, 6.0, ((0, 8), (1, 4))),
        "w_in": bell_draw(streams_of[1], (D, 3, D), D ** -0.5, 0.09375, ((2, 4),)),
        "short_filter": bell_draw(streams_of[2], (SHORT, 3, D), 0.6, 3.0, ((2, 4),), jnp.float32),
        "mr_filter": bell_draw(streams_of[3], (GROUPS, LEN), LEN ** -0.5, 0.5, ((0, 4),)),
        "skip_gain": bell_draw(streams_of[4], (D,), 1.0, 4.0, ((0, 4),), jnp.float32),
        "w_out": bell_draw(streams_of[5], (D, D), D ** -0.5, 0.09375, ((0, 4),)),
        "segments": jnp.searchsorted(jnp.cumsum(ragged(streams_of[6], DOCS, TOKENS, TOKENS // 8, 2)), jnp.arange(TOKENS), side="right").astype(jnp.int32),
    }


def unfold(folded):
    rest = folded.shape[1:]
    period_parts = folded.reshape((N_SEQ, TOKENS // (2 * N_SEQ), 2) + rest)
    first_slot = jnp.swapaxes(period_parts[:, :, 0], 0, 1)
    second = jnp.swapaxes(period_parts[::-1, :, 1], 0, 1)
    return jnp.concatenate([first_slot, second], axis=1).reshape((TOKENS,) + rest)


def refold(contiguous):
    rest = contiguous.shape[1:]
    period_parts = contiguous.reshape((TOKENS // (2 * N_SEQ), 2, N_SEQ) + rest)
    first_slot = period_parts[:, 0]
    second = period_parts[:, 1][:, ::-1]
    stacked = jnp.stack([first_slot, second], axis=2)
    return jnp.swapaxes(stacked, 0, 1).reshape((TOKENS,) + rest)


def short_conv(extended, seg_ext, weights):
    short_taps = weights.shape[0]
    row_count = extended.shape[0] - short_taps + 1
    seg_own = seg_ext[short_taps - 1:]
    tail_shape = (row_count,) + (1,) * (extended.ndim - 1)
    running = jnp.zeros((row_count,) + extended.shape[1:], jnp.float32)
    for tap_index in range(short_taps):
        lead_rows = short_taps - 1 - tap_index
        shifted = extended[lead_rows:lead_rows + row_count].astype(jnp.float32)
        same_doc = (seg_ext[lead_rows:lead_rows + row_count] == seg_own).astype(jnp.float32)
        running = running + weights[tap_index].astype(jnp.float32) * shifted * same_doc.reshape(tail_shape)
    return running


def band_matrix(filters):
    groups, tap_count = filters.shape
    flipped = filters[:, ::-1]
    blank = jnp.zeros((groups, tap_count), filters.dtype)
    row_pattern = jnp.concatenate([blank, flipped, blank], axis=1)
    tiled_rows = jnp.tile(row_pattern, (1, tap_count))
    tiled_rows = jnp.concatenate([tiled_rows, blank], axis=1)
    shaped = tiled_rows.reshape(groups, tap_count, 3 * tap_count + 1)[:, :, :2 * tap_count]
    return shaped[:, ::-1, :]


def long_conv(gated, band_mats, segments):
    tap_count = band_mats.shape[1]
    lead_block = jnp.zeros((tap_count,) + gated.shape[1:], gated.dtype)
    extended = jnp.concatenate([lead_block, gated])
    seg_ext = jnp.concatenate([jnp.full((tap_count,), -1, jnp.int32), segments])
    band_wide = band_mats.astype(jnp.float32)

    def one_block(block_index):
        offset = (block_index * tap_count).astype(jnp.int32)
        window = lax.dynamic_slice_in_dim(extended, offset, 2 * tap_count, 0).astype(jnp.float32)
        seg_window = lax.dynamic_slice_in_dim(seg_ext, offset, 2 * tap_count, 0)
        seg_own = lax.dynamic_slice_in_dim(seg_ext, offset + tap_count, tap_count, 0)
        doc_mask = seg_own[:, None] == seg_window[None, :]
        masked = jnp.where(doc_mask[None], band_wide, jnp.zeros((), band_wide.dtype))
        return jnp.einsum('gab,bgc->agc', masked, window)

    blocks_out = lax.map(one_block, jnp.arange(TOKENS // tap_count, dtype=jnp.int32))
    return blocks_out.reshape(gated.shape)


def reference(tokens, w_in, short_filter, mr_filter, skip_gain, w_out, segments):
    flat_in = w_in.reshape(D, 3 * D)
    projected = jnp.dot(tokens, flat_in, preferred_element_type=jnp.float32).astype(jnp.bfloat16)
    qkv = unfold(projected.reshape(TOKENS, 3, D))
    lead_rows = SHORT - 1
    extended = jnp.concatenate([jnp.zeros((lead_rows, 3, D), jnp.bfloat16), qkv])
    seg_ext = jnp.concatenate([jnp.full((lead_rows,), -1, jnp.int32), segments])
    convolved = short_conv(extended, seg_ext, short_filter)
    gated_in = (convolved[:, 1] * convolved[:, 2]).astype(jnp.bfloat16)
    band_mats = band_matrix(mr_filter)
    long_out = long_conv(gated_in.reshape(TOKENS, GROUPS, GSIZE), band_mats, segments).reshape(TOKENS, D)
    gated_out = (convolved[:, 0] * (long_out + skip_gain * gated_in.astype(jnp.float32))).astype(jnp.bfloat16)
    folded_out = refold(gated_out)
    return jnp.dot(folded_out, w_out, preferred_element_type=jnp.float32).astype(jnp.bfloat16)
```

```python
import functools

import jax
import jax.numpy as jnp
from jax import lax
from jax.experimental import pallas as pl
from jax.experimental.pallas import tpu as pltpu
from jax.sharding import PartitionSpec as P

LANES = 128
PACK = 16


def fold_matrix(row_count, seq_count):
    periods = row_count // (2 * seq_count)
    out_row = lax.broadcasted_iota(jnp.int32, (row_count, row_count), 0)
    in_row = lax.broadcasted_iota(jnp.int32, (row_count, row_count), 1)
    d = out_row // (2 * periods)
    a = (out_row // 2) % periods
    s = out_row % 2
    wanted = a * 2 * seq_count + jnp.where(s == 0, d, 2 * seq_count - 1 - d)
    return (wanted == in_row).astype(jnp.bfloat16)


def short_conv(x, weights, masks, start):
    rows = x.shape[0] - start
    total = weights[0:1] * x[start:]
    for j in range(1, weights.shape[0]):
        total = total + weights[j : j + 1] * x[start - j : start - j + rows] * masks[:, j : j + 1]
    return total


def mix_kernel(
    gsize, q, k, v, hq, hk, hv, short, pattern, skip, near, seg_col, seg_row, fold, out
):
    rows, lanes = q.shape
    taps = pattern.shape[1] // 2
    groups = lanes // gsize
    f32 = jnp.float32
    masks = near[...]
    qx = jnp.concatenate([hq[...].astype(f32), q[...].astype(f32)])
    kx = jnp.concatenate([hk[...].astype(f32), k[...].astype(f32)])
    vx = jnp.concatenate([hv[...].astype(f32), v[...].astype(f32)])
    sq = short_conv(qx, short[:, 0], masks[taps:], hq.shape[0])
    sk = short_conv(kx, short[:, 1], masks, hk.shape[0] - taps)
    sv = short_conv(vx, short[:, 2], masks, hk.shape[0] - taps)
    gated = (sk * sv).astype(jnp.bfloat16)
    lane_group = lax.broadcasted_iota(jnp.int32, (taps, lanes), 1) // gsize
    bands = []
    for g in range(groups):
        row = jnp.broadcast_to(pattern[g : g + 1], (taps, 2 * taps))
        bands.append(pltpu.roll(row, 0, 1, stride=1, stride_axis=0))
    parts = []
    for b in range(rows // taps):
        same = seg_col[b * taps : (b + 1) * taps] == seg_row[:, b * taps : (b + 2) * taps]
        lhs = jnp.concatenate(
            [jnp.where(same, band, 0.0).astype(jnp.bfloat16) for band in bands]
        )
        window = gated[b * taps : (b + 2) * taps]
        every = jnp.dot(lhs, window, preferred_element_type=f32)
        total = jnp.zeros((taps, lanes), f32)
        for g in range(groups):
            total = jnp.where(lane_group == g, every[g * taps : (g + 1) * taps], total)
        parts.append(total)
    long_out = jnp.concatenate(parts)
    mixed = (sq * (long_out + skip[...] * gated[taps:].astype(f32))).astype(jnp.bfloat16)
    out[...] = jnp.dot(fold[...], mixed, preferred_element_type=f32).astype(jnp.bfloat16)


def mix(qkv, halos, short_filter, mr_filter, skip_gain, segments, fold):
    rows, chans = qkv[0].shape
    groups, taps = mr_filter.shape
    short_taps = short_filter.shape[0]
    gsize = chans // groups
    per = LANES // gsize
    base = lax.axis_index("seq") * rows
    lead = halos[1].shape[0]
    padded = jnp.concatenate([jnp.full((lead,), -1, jnp.int32), segments])
    ext = lax.dynamic_slice_in_dim(padded, base, rows + lead, 0)
    window = ext[lead - taps :]
    near = jnp.stack(
        [
            (ext[lead - taps - j : rows + lead - j] == window).astype(jnp.float32)
            for j in range(short_taps)
        ],
        axis=1,
    )
    pattern = jnp.pad(mr_filter[:, ::-1].astype(jnp.float32), ((0, 0), (1, taps - 1)))
    whole = lambda shape: pl.BlockSpec(shape, lambda i: (0, 0))
    lane = lambda height: pl.BlockSpec((height, LANES), lambda i: (0, i))
    return pl.pallas_call(
        functools.partial(mix_kernel, gsize),
        grid=(chans // LANES,),
        out_shape=jax.ShapeDtypeStruct((rows, chans), jnp.bfloat16),
        in_specs=[lane(rows)] * 3
        + [lane(h.shape[0]) for h in halos]
        + [
            pl.BlockSpec((short_taps, 3, LANES), lambda i: (0, 0, i)),
            pl.BlockSpec((per, 2 * taps), lambda i: (i, 0)),
            lane(1),
            whole(near.shape),
            whole((rows, 1)),
            whole((1, rows + taps)),
            whole(fold.shape),
        ],
        out_specs=lane(rows),
        compiler_params=pltpu.CompilerParams(vmem_limit_bytes=32 * 2**20),
    )(
        *qkv,
        *halos,
        short_filter,
        pattern,
        skip_gain[None],
        near,
        ext[lead:, None],
        window[None],
        fold,
    )


def body(tokens, w_in, short_filter, mr_filter, skip_gain, w_out, segments):
    rows, width = tokens.shape
    seq_count = lax.axis_size("seq")
    taps = mr_filter.shape[1]
    fold = fold_matrix(rows, seq_count)
    pieces = tokens.reshape(seq_count, rows // seq_count, width)
    received = lax.all_to_all(pieces, "seq", split_axis=0, concat_axis=0, tiled=True)
    ordered = lax.dot_general(
        fold,
        received.reshape(rows, width),
        (((0,), (0,)), ((), ())),
        preferred_element_type=jnp.float32,
    ).astype(jnp.bfloat16)
    gathered = lax.all_gather(ordered, "chan", axis=1, tiled=True)
    q, k, v = [
        jnp.dot(gathered, w_in[:, i], preferred_element_type=jnp.float32).astype(jnp.bfloat16)
        for i in range(3)
    ]
    tails = (q[rows - PACK :], k[rows - taps - PACK :], v[rows - taps - PACK :])
    ring = [(i, i + 1) for i in range(seq_count - 1)]
    halos = lax.ppermute(tails, "seq", ring)
    folded = mix((q, k, v), halos, short_filter, mr_filter, skip_gain, segments, fold)
    outgoing = folded.reshape(seq_count, rows // seq_count, folded.shape[1])
    returned = lax.all_to_all(outgoing, "seq", split_axis=0, concat_axis=0, tiled=True)
    partial = jnp.dot(
        returned.reshape(rows, -1), w_out, preferred_element_type=jnp.float32
    ).astype(jnp.bfloat16)
    return lax.psum_scatter(partial, "chan", scatter_dimension=1, tiled=True)


def solution(mesh):
    return jax.shard_map(
        body,
        mesh=mesh,
        in_specs=(
            P("seq", "chan"),
            P(None, None, "chan"),
            P(None, None, "chan"),
            P("chan", None),
            P("chan"),
            P("chan", None),
            P(),
        ),
        out_specs=P("seq", "chan"),
        check_vma=False,
    )
```

```python
import functools

import jax
import jax.numpy as jnp
from jax import lax
from jax.experimental import pallas as pl
from jax.experimental.pallas import tpu as pltpu
from jax.sharding import PartitionSpec as P

LANES = 128
PACK = 16


def fold_matrix(row_count, seq_count):
    periods = row_count // (2 * seq_count)
    out_row = lax.broadcasted_iota(jnp.int32, (row_count, row_count), 0)
    in_row = lax.broadcasted_iota(jnp.int32, (row_count, row_count), 1)
    d = out_row // (2 * periods)
    a = (out_row // 2) % periods
    s = out_row % 2
    wanted = a * 2 * seq_count + jnp.where(s == 0, d, 2 * seq_count - 1 - d)
    return (wanted == in_row).astype(jnp.bfloat16)


def short_conv(x, weights, masks, start):
    rows = x.shape[0] - start
    total = weights[0:1] * x[start:]
    for j in range(1, weights.shape[0]):
        total = total + weights[j : j + 1] * x[start - j : start - j + rows] * masks[:, j : j + 1]
    return total


def mix_kernel(
    gsize, q, k, v, hq, hk, hv, short, pattern, skip, near, seg_col, seg_row, fold, out
):
    rows, lanes = q.shape
    taps = pattern.shape[1] // 2
    groups = lanes // gsize
    f32 = jnp.float32
    masks = near[...]
    qx = jnp.concatenate([hq[...].astype(f32), q[...].astype(f32)])
    kx = jnp.concatenate([hk[...].astype(f32), k[...].astype(f32)])
    vx = jnp.concatenate([hv[...].astype(f32), v[...].astype(f32)])
    sq = short_conv(qx, short[:, 0], masks[taps:], hq.shape[0])
    sk = short_conv(kx, short[:, 1], masks, hk.shape[0] - taps)
    sv = short_conv(vx, short[:, 2], masks, hk.shape[0] - taps)
    gated = (sk * sv).astype(jnp.bfloat16)
    lane_group = lax.broadcasted_iota(jnp.int32, (taps, lanes), 1) // gsize
    bands = []
    for g in range(groups):
        row = jnp.broadcast_to(pattern[g : g + 1], (taps, 2 * taps))
        bands.append(pltpu.roll(row, 0, 1, stride=1, stride_axis=0))
    parts = []
    for b in range(rows // taps):
        same = seg_col[b * taps : (b + 1) * taps] == seg_row[:, b * taps : (b + 2) * taps]
        lhs = jnp.concatenate(
            [jnp.where(same, band, 0.0).astype(jnp.bfloat16) for band in bands]
        )
        window = gated[b * taps : (b + 2) * taps]
        every = jnp.dot(lhs, window, preferred_element_type=f32)
        total = jnp.zeros((taps, lanes), f32)
        for g in range(groups):
            total = jnp.where(lane_group == g, every[g * taps : (g + 1) * taps], total)
        parts.append(total)
    long_out = jnp.concatenate(parts)
    mixed = (sq * (long_out + skip[...] * gated[taps:].astype(f32))).astype(jnp.bfloat16)
    out[...] = jnp.dot(fold[...], mixed, preferred_element_type=f32).astype(jnp.bfloat16)


def mix(qkv, halos, short_filter, mr_filter, skip_gain, segments, fold):
    rows, chans = qkv[0].shape
    groups, taps = mr_filter.shape
    short_taps = short_filter.shape[0]
    gsize = chans // groups
    per = LANES // gsize
    base = lax.axis_index("seq") * rows
    lead = halos[1].shape[0]
    padded = jnp.concatenate([jnp.full((lead,), -1, jnp.int32), segments])
    ext = lax.dynamic_slice_in_dim(padded, base, rows + lead, 0)
    window = ext[lead - taps :]
    near = jnp.stack(
        [
            (ext[lead - taps - j : rows + lead - j] == window).astype(jnp.float32)
            for j in range(short_taps)
        ],
        axis=1,
    )
    pattern = jnp.pad(mr_filter[:, ::-1].astype(jnp.float32), ((0, 0), (1, taps - 1)))
    whole = lambda shape: pl.BlockSpec(shape, lambda i: (0, 0))
    lane = lambda height: pl.BlockSpec((height, LANES), lambda i: (0, i))
    return pl.pallas_call(
        functools.partial(mix_kernel, gsize),
        grid=(chans // LANES,),
        out_shape=jax.ShapeDtypeStruct((rows, chans), jnp.bfloat16),
        in_specs=[lane(rows)] * 3
        + [lane(h.shape[0]) for h in halos]
        + [
            pl.BlockSpec((short_taps, 3, LANES), lambda i: (0, 0, i)),
            pl.BlockSpec((per, 2 * taps), lambda i: (i, 0)),
            lane(1),
            whole(near.shape),
            whole((rows, 1)),
            whole((1, rows + taps)),
            whole(fold.shape),
        ],
        out_specs=lane(rows),
        compiler_params=pltpu.CompilerParams(vmem_limit_bytes=32 * 2**20),
    )(
        *qkv,
        *halos,
        short_filter,
        pattern,
        skip_gain[None],
        near,
        ext[lead:, None],
        window[None],
        fold,
    )


def remote(src, dst, sems, index, device):
    send, recv = sems
    return pltpu.make_async_remote_copy(
        src_ref=src,
        dst_ref=dst,
        send_sem=send.at[index],
        recv_sem=recv.at[index],
        device_id=device,
        device_id_type=pl.DeviceIdType.MESH,
    )


def place(seq_count, chan_count):
    chan = lax.axis_index("chan")
    return lax.axis_index("seq"), chan // 2, chan % 2, chan_count // 2


def greet(devices):
    barrier = pltpu.get_barrier_semaphore()
    for device in devices:
        pl.semaphore_signal(
            barrier, inc=1, device_id=device, device_id_type=pl.DeviceIdType.MESH
        )
    pl.semaphore_wait(barrier, len(devices))


def partners(seq, chip, core, seq_count, chips):
    rows = [{"seq": lax.rem(seq + o, seq_count)} for o in range(1, seq_count)]
    across = [{"chan": lax.rem(chip + o, chips) * 2 + core} for o in range(1, chips)]
    return rows, across, {"chan": chip * 2 + 1 - core}


def exchange_rows(source, target, sems, seq, devices):
    count = len(devices) + 1
    piece = source.shape[0] // count
    at = lambda ref, d: ref.at[pl.ds(pl.multiple_of(d * piece, piece), piece)]
    copies = []
    for o in range(1, count):
        d = lax.rem(seq + o, count)
        copies.append(remote(at(source, d), at(target, seq), sems, o - 1, devices[o - 1]))
        copies[-1].start()
    at(target, seq)[...] = at(source, seq)[...]
    return copies


def project_kernel(
    seq_count, chan_count, tokens, w, order, q, k, v, hq, hk, hv,
    landed, blocks, wbuf, total, row_send, row_recv, col_send, col_recv, halo_send, halo_recv, w_sem,
):
    seq, chip, core, chips = place(seq_count, chan_count)
    rows_to, across, sibling = partners(seq, chip, core, seq_count, chips)
    width = tokens.shape[1]
    f32 = jnp.float32
    tile = min(256, wbuf.shape[2])
    tiles = wbuf.shape[2] // tile

    uses = [chip * 2 + core, chip * 2 + 1 - core]
    for o in range(1, chips):
        origin = lax.rem(chip - o + chips, chips)
        uses += [origin * 2 + core, origin * 2 + 1 - core]
    part = lambda c: pl.ds(pl.multiple_of(c * width, width), width)
    loads = []
    for n, c in enumerate(uses):
        loads.append(
            pltpu.make_async_copy(w.at[:, part(c)], wbuf.at[:, part(c)], w_sem.at[n])
        )
        loads[-1].start()

    greet(rows_to + across + [sibling])
    copies = exchange_rows(tokens, landed, (row_send, row_recv), seq, rows_to)
    for copy in copies:
        copy.wait()
    mine = uses[0]
    blocks[mine] = jnp.dot(order[...], landed[...], preferred_element_type=f32).astype(
        jnp.bfloat16
    )
    sems = (col_send, col_recv)
    outs = [
        remote(blocks.at[mine], blocks.at[mine], sems, o, across[o - 1])
        for o in range(1, chips)
    ]
    inner = remote(blocks.at[mine], blocks.at[mine], sems, 0, sibling)
    for copy in outs + [inner]:
        copy.start()

    def multiply(n):
        c = uses[n]
        loads[n].wait()

        @pl.loop(0, 3 * tiles)
        def _(t):
            i = lax.div(t, tiles)
            cols = pl.ds(pl.multiple_of(lax.rem(t, tiles) * tile, tile), tile)
            term = jnp.dot(blocks[c], wbuf[i, part(c), cols], preferred_element_type=f32)
            if n == 0:
                total[i, :, cols] = term
            else:
                total[i, :, cols] += term

    multiply(0)
    inner.wait_recv()
    multiply(1)
    for o in range(1, chips):
        outs[o - 1].wait_recv()
        c = uses[2 * o]
        forward = remote(blocks.at[c], blocks.at[c], sems, chips - 1 + o, sibling)
        forward.start()
        multiply(2 * o)
        forward.wait()
        multiply(2 * o + 1)
    for copy in outs + [inner]:
        copy.wait_send()
    halos = []
    after = rows_to[0]
    for i, (ref, halo) in enumerate(((q, hq), (k, hk), (v, hv))):
        ref[...] = total[i].astype(jnp.bfloat16)
        tail = halo.shape[0]
        src = ref.at[pl.ds(ref.shape[0] - tail, tail)]
        halos.append(remote(src, halo, (halo_send, halo_recv), i, after))
        halos[-1].start()
    for copy in halos:
        copy.wait()


def project(tokens, w_in, order, taps, seq_count, chan_count):
    rows, width = tokens.shape
    chans = w_in.shape[2]
    vmem = pl.BlockSpec(memory_space=pltpu.VMEM)
    bf16 = jnp.bfloat16
    dma = pltpu.SemaphoreType.DMA
    shape = lambda height: jax.ShapeDtypeStruct((height, chans), bf16)
    return pl.pallas_call(
        functools.partial(project_kernel, seq_count, chan_count),
        out_shape=[shape(rows)] * 3 + [shape(PACK)] + [shape(taps + PACK)] * 2,
        in_specs=[vmem, pl.BlockSpec(memory_space=pl.ANY), vmem],
        out_specs=[vmem] * 6,
        scratch_shapes=[
            pltpu.VMEM((rows, width), bf16),
            pltpu.VMEM((chan_count, rows, width), bf16),
            pltpu.VMEM((3, w_in.shape[0], chans), bf16),
            pltpu.VMEM((3, rows, chans), jnp.float32),
            dma((seq_count - 1,)),
            dma((seq_count - 1,)),
            dma((chan_count - 1,)),
            dma((chan_count - 1,)),
            dma((3,)),
            dma((3,)),
            dma((chan_count,)),
        ],
        compiler_params=pltpu.CompilerParams(
            collective_id=0, has_side_effects=True, vmem_limit_bytes=48 * 2**20
        ),
    )(tokens, jnp.swapaxes(w_in, 0, 1), order)


def output_kernel(
    seq_count, chan_count, folded, w, out,
    landed, wbuf, kept, inner_out, inner_in, across_out, across_in,
    row_send, row_recv, inner_send, inner_recv, across_send, across_recv, w_sem,
):
    seq, chip, core, chips = place(seq_count, chan_count)
    rows_to, across, sibling = partners(seq, chip, core, seq_count, chips)
    f32 = jnp.float32
    width = out.shape[1]
    tile = min(256, width)
    load = pltpu.make_async_copy(w, wbuf, w_sem)
    load.start()
    greet(rows_to + across + [sibling])
    copies = exchange_rows(folded, landed, (row_send, row_recv), seq, rows_to)
    for copy in copies:
        copy.wait()
    load.wait()

    def multiply(c, target, slot):
        @pl.loop(0, width // tile)
        def _(t):
            start = pl.multiple_of(t * tile, tile)
            cols = pl.ds(pl.multiple_of(c * width + start, tile), tile)
            term = jnp.dot(landed[...], wbuf[:, cols], preferred_element_type=f32)
            target[slot, :, pl.ds(start, tile)] = term.astype(target.dtype)

    inners = []

    def share(c, slot):
        multiply(c * 2 + 1 - core, inner_out, slot)
        inners.append(
            remote(inner_out.at[slot], inner_in.at[slot], (inner_send, inner_recv), slot, sibling)
        )
        inners[-1].start()
        multiply(c * 2 + core, kept, slot)

    outs = []
    for o in range(1, chips):
        share(lax.rem(chip + o, chips), o - 1)
        inners[-1].wait_recv()
        across_out[o - 1] = (kept[o - 1] + inner_in[o - 1].astype(f32)).astype(jnp.bfloat16)
        outs.append(
            remote(
                across_out.at[o - 1], across_in.at[o - 1], (across_send, across_recv), o - 1,
                across[o - 1],
            )
        )
        outs[-1].start()
    share(chip, chips - 1)
    inners[-1].wait_recv()
    kept[chips - 1] += inner_in[chips - 1].astype(f32)
    result = kept[chips - 1]
    for o in range(1, chips):
        outs[o - 1].wait_recv()
        result = result + across_in[o - 1].astype(f32)
    out[...] = result.astype(out.dtype)
    for copy in inners + outs:
        copy.wait_send()


def project_out(folded, w_out, seq_count, chan_count):
    rows, chans = folded.shape
    width = w_out.shape[1] // chan_count
    chips = chan_count // 2
    vmem = pl.BlockSpec(memory_space=pltpu.VMEM)
    bf16 = jnp.bfloat16
    dma = pltpu.SemaphoreType.DMA
    slots = lambda count: pltpu.VMEM((count, rows, width), bf16)
    return pl.pallas_call(
        functools.partial(output_kernel, seq_count, chan_count),
        out_shape=jax.ShapeDtypeStruct((rows, width), bf16),
        in_specs=[vmem, pl.BlockSpec(memory_space=pl.ANY)],
        out_specs=vmem,
        scratch_shapes=[
            pltpu.VMEM((rows, chans), bf16),
            pltpu.VMEM(w_out.shape, bf16),
            pltpu.VMEM((chips, rows, width), jnp.float32),
            slots(chips),
            slots(chips),
            slots(chips - 1),
            slots(chips - 1),
            dma((seq_count - 1,)),
            dma((seq_count - 1,)),
            dma((chips,)),
            dma((chips,)),
            dma((chips - 1,)),
            dma((chips - 1,)),
            dma(()),
        ],
        compiler_params=pltpu.CompilerParams(
            collective_id=1, has_side_effects=True, vmem_limit_bytes=32 * 2**20
        ),
    )(folded, w_out)


def body(tokens, w_in, short_filter, mr_filter, skip_gain, w_out, segments):
    rows, width = tokens.shape
    seq_count = lax.axis_size("seq")
    taps = mr_filter.shape[1]
    fold = fold_matrix(rows, seq_count)
    chan_size = lax.axis_size("chan")
    if rows // seq_count % PACK == 0 and chan_size % 2 == 0 and chan_size > 2:
        q, k, v, *halos = project(tokens, w_in, fold.T, taps, seq_count, chan_size)
        folded = mix((q, k, v), halos, short_filter, mr_filter, skip_gain, segments, fold)
        return project_out(folded, w_out, seq_count, chan_size)
    pieces = tokens.reshape(seq_count, rows // seq_count, width)
    received = lax.all_to_all(pieces, "seq", split_axis=0, concat_axis=0, tiled=True)
    ordered = lax.dot_general(
        fold,
        received.reshape(rows, width),
        (((0,), (0,)), ((), ())),
        preferred_element_type=jnp.float32,
    ).astype(jnp.bfloat16)
    gathered = lax.all_gather(ordered, "chan", axis=1, tiled=True)
    q, k, v = [
        jnp.dot(gathered, w_in[:, i], preferred_element_type=jnp.float32).astype(jnp.bfloat16)
        for i in range(3)
    ]
    tails = (q[rows - PACK :], k[rows - taps - PACK :], v[rows - taps - PACK :])
    ring = [(i, i + 1) for i in range(seq_count - 1)]
    halos = lax.ppermute(tails, "seq", ring)
    folded = mix((q, k, v), halos, short_filter, mr_filter, skip_gain, segments, fold)
    outgoing = folded.reshape(seq_count, rows // seq_count, folded.shape[1])
    returned = lax.all_to_all(outgoing, "seq", split_axis=0, concat_axis=0, tiled=True)
    partial = jnp.dot(
        returned.reshape(rows, -1), w_out, preferred_element_type=jnp.float32
    ).astype(jnp.bfloat16)
    return lax.psum_scatter(partial, "chan", scatter_dimension=1, tiled=True)


def solution(mesh):
    return jax.shard_map(
        body,
        mesh=mesh,
        in_specs=(
            P("seq", "chan"),
            P(None, None, "chan"),
            P(None, None, "chan"),
            P("chan", None),
            P("chan"),
            P("chan", None),
            P(),
        ),
        out_specs=P("seq", "chan"),
        check_vma=False,
    )
```

```python
import functools

import jax
import jax.numpy as jnp
from jax import lax
from jax.experimental import pallas as pl
from jax.experimental.pallas import tpu as pltpu
from jax.sharding import PartitionSpec as P

LANES = 128
PACK = 16


def fold_matrix(row_count, seq_count):
    periods = row_count // (2 * seq_count)
    out_row = lax.broadcasted_iota(jnp.int32, (row_count, row_count), 0)
    in_row = lax.broadcasted_iota(jnp.int32, (row_count, row_count), 1)
    d = out_row // (2 * periods)
    a = (out_row // 2) % periods
    s = out_row % 2
    wanted = a * 2 * seq_count + jnp.where(s == 0, d, 2 * seq_count - 1 - d)
    return (wanted == in_row).astype(jnp.bfloat16)


def short_conv(x, weights, masks, start):
    rows = x.shape[0] - start
    total = weights[0:1] * x[start:]
    for j in range(1, weights.shape[0]):
        total = total + weights[j : j + 1] * x[start - j : start - j + rows] * masks[:, j : j + 1]
    return total


def mix_kernel(
    gsize, q, k, v, hq, hk, hv, short, pattern, skip, near, seg_col, seg_row, fold, out
):
    rows, lanes = q.shape
    taps = pattern.shape[1] // 2
    groups = lanes // gsize
    f32 = jnp.float32
    masks = near[...]
    qx = jnp.concatenate([hq[...].astype(f32), q[...].astype(f32)])
    kx = jnp.concatenate([hk[...].astype(f32), k[...].astype(f32)])
    vx = jnp.concatenate([hv[...].astype(f32), v[...].astype(f32)])
    sq = short_conv(qx, short[:, 0], masks[taps:], hq.shape[0])
    sk = short_conv(kx, short[:, 1], masks, hk.shape[0] - taps)
    sv = short_conv(vx, short[:, 2], masks, hk.shape[0] - taps)
    gated = (sk * sv).astype(jnp.bfloat16)
    lane_group = lax.broadcasted_iota(jnp.int32, (taps, lanes), 1) // gsize
    bands = []
    for g in range(groups):
        row = jnp.broadcast_to(pattern[g : g + 1], (taps, 2 * taps))
        bands.append(pltpu.roll(row, 0, 1, stride=1, stride_axis=0))
    parts = []
    for b in range(rows // taps):
        same = seg_col[b * taps : (b + 1) * taps] == seg_row[:, b * taps : (b + 2) * taps]
        lhs = jnp.concatenate(
            [jnp.where(same, band, 0.0).astype(jnp.bfloat16) for band in bands]
        )
        window = gated[b * taps : (b + 2) * taps]
        every = jnp.dot(lhs, window, preferred_element_type=f32)
        total = jnp.zeros((taps, lanes), f32)
        for g in range(groups):
            total = jnp.where(lane_group == g, every[g * taps : (g + 1) * taps], total)
        parts.append(total)
    long_out = jnp.concatenate(parts)
    mixed = (sq * (long_out + skip[...] * gated[taps:].astype(f32))).astype(jnp.bfloat16)
    out[...] = jnp.dot(fold[...], mixed, preferred_element_type=f32).astype(jnp.bfloat16)


def mix(qkv, halos, short_filter, mr_filter, skip_gain, segments, fold):
    rows, chans = qkv[0].shape
    groups, taps = mr_filter.shape
    short_taps = short_filter.shape[0]
    gsize = chans // groups
    per = LANES // gsize
    base = lax.axis_index("seq") * rows
    lead = halos[1].shape[0]
    padded = jnp.concatenate([jnp.full((lead,), -1, jnp.int32), segments])
    ext = lax.dynamic_slice_in_dim(padded, base, rows + lead, 0)
    window = ext[lead - taps :]
    near = jnp.stack(
        [
            (ext[lead - taps - j : rows + lead - j] == window).astype(jnp.float32)
            for j in range(short_taps)
        ],
        axis=1,
    )
    pattern = jnp.pad(mr_filter[:, ::-1].astype(jnp.float32), ((0, 0), (1, taps - 1)))
    whole = lambda shape: pl.BlockSpec(shape, lambda i: (0, 0))
    lane = lambda height: pl.BlockSpec((height, LANES), lambda i: (0, i))
    return pl.pallas_call(
        functools.partial(mix_kernel, gsize),
        grid=(chans // LANES,),
        out_shape=jax.ShapeDtypeStruct((rows, chans), jnp.bfloat16),
        in_specs=[lane(rows)] * 3
        + [lane(h.shape[0]) for h in halos]
        + [
            pl.BlockSpec((short_taps, 3, LANES), lambda i: (0, 0, i)),
            pl.BlockSpec((per, 2 * taps), lambda i: (i, 0)),
            lane(1),
            whole(near.shape),
            whole((rows, 1)),
            whole((1, rows + taps)),
            whole(fold.shape),
        ],
        out_specs=lane(rows),
        compiler_params=pltpu.CompilerParams(vmem_limit_bytes=32 * 2**20),
    )(
        *qkv,
        *halos,
        short_filter,
        pattern,
        skip_gain[None],
        near,
        ext[lead:, None],
        window[None],
        fold,
    )


def remote(src, dst, sems, index, device):
    send, recv = sems
    return pltpu.make_async_remote_copy(
        src_ref=src,
        dst_ref=dst,
        send_sem=send.at[index],
        recv_sem=recv.at[index],
        device_id=device,
        device_id_type=pl.DeviceIdType.MESH,
    )


def place(seq_count, chan_count):
    chan = lax.axis_index("chan")
    return lax.axis_index("seq"), chan // 2, chan % 2, chan_count // 2


def greet(devices):
    barrier = pltpu.get_barrier_semaphore()
    for device in devices:
        pl.semaphore_signal(
            barrier, inc=1, device_id=device, device_id_type=pl.DeviceIdType.MESH
        )
    pl.semaphore_wait(barrier, len(devices))


def partners(seq, chip, core, seq_count, chips):
    rows = [{"seq": lax.rem(seq + o, seq_count)} for o in range(1, seq_count)]
    across = [{"chan": lax.rem(chip + o, chips) * 2 + core} for o in range(1, chips)]
    return rows, across, {"chan": chip * 2 + 1 - core}


HALVES = (1, 0)


def exchange_rows(source, target, sems, seq, devices, half):
    count = len(devices) + 1
    piece = source.shape[0] // count
    part = piece // 2
    take = lambda d: source.at[pl.ds(pl.multiple_of(d * piece + half * part, part), part)]
    put = target.at[half, pl.ds(pl.multiple_of(seq * part, part), part)]
    copies = []
    for o in range(1, count):
        index = half * (count - 1) + o - 1
        copies.append(remote(take(lax.rem(seq + o, count)), put, sems, index, devices[o - 1]))
        copies[-1].start()
    put[...] = take(seq)[...]
    return copies


def project_kernel(
    seq_count, chan_count, tokens, w, order, q, k, v, hq, hk, hv,
    landed, blocks, wbuf, total, row_send, row_recv, col_send, col_recv, halo_send, halo_recv, w_sem,
):
    seq, chip, core, chips = place(seq_count, chan_count)
    rows_to, across, sibling = partners(seq, chip, core, seq_count, chips)
    rows, width = tokens.shape
    half_rows = rows // 2
    f32 = jnp.float32
    tile = min(256, wbuf.shape[2])
    tiles = wbuf.shape[2] // tile

    uses = [chip * 2 + core, chip * 2 + 1 - core]
    for o in range(1, chips):
        origin = lax.rem(chip - o + chips, chips)
        uses += [origin * 2 + core, origin * 2 + 1 - core]
    part = lambda c: pl.ds(pl.multiple_of(c * width, width), width)
    loads = []
    for n, c in enumerate(uses):
        loads.append(
            pltpu.make_async_copy(w.at[:, part(c)], wbuf.at[:, part(c)], w_sem.at[n])
        )
        loads[-1].start()

    greet(rows_to + across + [sibling])
    row_sems = (row_send, row_recv)
    copies = {h: exchange_rows(tokens, landed, row_sems, seq, rows_to, h) for h in HALVES}
    mine = uses[0]
    sems = (col_send, col_recv)
    outs, inner = {}, {}

    def spread(h):
        for copy in copies[h]:
            copy.wait()
        own = blocks.at[h, mine]
        own[...] = jnp.dot(order[...], landed[h], preferred_element_type=f32).astype(jnp.bfloat16)
        first = h * (chan_count - 1)
        outs[h] = [remote(own, own, sems, first + o, across[o - 1]) for o in range(1, chips)]
        inner[h] = remote(own, own, sems, first, sibling)
        for copy in outs[h] + [inner[h]]:
            copy.start()

    def multiply(h, n):
        c = uses[n]
        if h == HALVES[0]:
            loads[n].wait()

        @pl.loop(0, 3 * tiles)
        def _(t):
            i = lax.div(t, tiles)
            cols = pl.ds(pl.multiple_of(lax.rem(t, tiles) * tile, tile), tile)
            term = jnp.dot(blocks[h, c], wbuf[i, part(c), cols], preferred_element_type=f32)
            if n == 0:
                total[i, :, cols] = term
            else:
                total[i, :, cols] += term

    def gather(h):
        inner[h].wait_recv()
        multiply(h, 1)
        for o in range(1, chips):
            outs[h][o - 1].wait_recv()
            own = blocks.at[h, uses[2 * o]]
            forward = remote(own, own, sems, h * (chan_count - 1) + chips - 1 + o, sibling)
            forward.start()
            multiply(h, 2 * o)
            forward.wait()
            multiply(h, 2 * o + 1)
        for i, ref in enumerate((q, k, v)):
            ref[pl.ds(h * half_rows, half_rows)] = total[i].astype(jnp.bfloat16)

    halos = []

    def send_halo(h):
        for i, (ref, halo) in enumerate(((q, hq), (k, hk), (v, hv))):
            lead = rows - halo.shape[0]
            start = max(lead, h * half_rows)
            size = (h + 1) * half_rows - start
            if size > 0:
                src = ref.at[pl.ds(start, size)]
                dst = halo.at[pl.ds(start - lead, size)]
                halos.append(remote(src, dst, (halo_send, halo_recv), h * 3 + i, rows_to[0]))
                halos[-1].start()

    spread(1)
    multiply(1, 0)
    spread(0)
    gather(1)
    send_halo(1)
    multiply(0, 0)
    gather(0)
    send_halo(0)
    for h in HALVES:
        for copy in outs[h] + [inner[h]]:
            copy.wait_send()
    for copy in halos:
        copy.wait()


def project(tokens, w_in, order, taps, seq_count, chan_count):
    rows, width = tokens.shape
    chans = w_in.shape[2]
    vmem = pl.BlockSpec(memory_space=pltpu.VMEM)
    bf16 = jnp.bfloat16
    dma = pltpu.SemaphoreType.DMA
    shape = lambda height: jax.ShapeDtypeStruct((height, chans), bf16)
    return pl.pallas_call(
        functools.partial(project_kernel, seq_count, chan_count),
        out_shape=[shape(rows)] * 3 + [shape(PACK)] + [shape(taps + PACK)] * 2,
        in_specs=[vmem, pl.BlockSpec(memory_space=pl.ANY), vmem],
        out_specs=[vmem] * 6,
        scratch_shapes=[
            pltpu.VMEM((2, rows // 2, width), bf16),
            pltpu.VMEM((2, chan_count, rows // 2, width), bf16),
            pltpu.VMEM((3, w_in.shape[0], chans), bf16),
            pltpu.VMEM((3, rows // 2, chans), jnp.float32),
            dma((2 * (seq_count - 1),)),
            dma((2 * (seq_count - 1),)),
            dma((2 * (chan_count - 1),)),
            dma((2 * (chan_count - 1),)),
            dma((6,)),
            dma((6,)),
            dma((chan_count,)),
        ],
        compiler_params=pltpu.CompilerParams(
            collective_id=0, has_side_effects=True, vmem_limit_bytes=48 * 2**20
        ),
    )(tokens, jnp.swapaxes(w_in, 0, 1), order)


def output_kernel(
    seq_count, chan_count, folded, w, out,
    landed, wbuf, kept, inner_out, inner_in, across_out, across_in,
    row_send, row_recv, inner_send, inner_recv, across_send, across_recv, w_sem,
):
    seq, chip, core, chips = place(seq_count, chan_count)
    rows_to, across, sibling = partners(seq, chip, core, seq_count, chips)
    f32 = jnp.float32
    width = out.shape[1]
    tile = min(256, width)
    load = pltpu.make_async_copy(w, wbuf, w_sem)
    load.start()
    greet(rows_to + across + [sibling])
    row_sems = (row_send, row_recv)
    copies = {h: exchange_rows(folded, landed, row_sems, seq, rows_to, h) for h in HALVES}

    def multiply(h, c, target, slot):
        @pl.loop(0, width // tile)
        def _(t):
            start = pl.multiple_of(t * tile, tile)
            cols = pl.ds(pl.multiple_of(c * width + start, tile), tile)
            term = jnp.dot(landed[h], wbuf[:, cols], preferred_element_type=f32)
            target[h, slot, :, pl.ds(start, tile)] = term.astype(target.dtype)

    inners, outs = {0: [], 1: []}, {0: [], 1: []}

    def share(h, c, slot):
        multiply(h, c * 2 + 1 - core, inner_out, slot)
        src, dst = inner_out.at[h, slot], inner_in.at[h, slot]
        index = h * chips + slot
        inners[h].append(remote(src, dst, (inner_send, inner_recv), index, sibling))
        inners[h][-1].start()
        multiply(h, c * 2 + core, kept, slot)

    for h in HALVES:
        for copy in copies[h]:
            copy.wait()
        if h == HALVES[0]:
            load.wait()
        for o in range(1, chips):
            n = o - 1
            share(h, lax.rem(chip + o, chips), n)
            inners[h][-1].wait_recv()
            across_out[h, n] = (kept[h, n] + inner_in[h, n].astype(f32)).astype(jnp.bfloat16)
            src, dst = across_out.at[h, n], across_in.at[h, n]
            index = h * (chips - 1) + n
            outs[h].append(remote(src, dst, (across_send, across_recv), index, across[n]))
            outs[h][-1].start()
        share(h, chip, chips - 1)

    part = landed.shape[1] // seq_count
    for h in HALVES:
        inners[h][-1].wait_recv()
        result = kept[h, chips - 1] + inner_in[h, chips - 1].astype(f32)
        for o in range(1, chips):
            outs[h][o - 1].wait_recv()
            result = result + across_in[h, o - 1].astype(f32)
        result = result.astype(out.dtype)
        for d in range(seq_count):
            out[pl.ds((2 * d + h) * part, part)] = result[d * part : (d + 1) * part]
    for h in HALVES:
        for copy in inners[h] + outs[h]:
            copy.wait_send()


def project_out(folded, w_out, seq_count, chan_count):
    rows, chans = folded.shape
    width = w_out.shape[1] // chan_count
    chips = chan_count // 2
    vmem = pl.BlockSpec(memory_space=pltpu.VMEM)
    bf16 = jnp.bfloat16
    dma = pltpu.SemaphoreType.DMA
    slots = lambda count: pltpu.VMEM((2, count, rows // 2, width), bf16)
    return pl.pallas_call(
        functools.partial(output_kernel, seq_count, chan_count),
        out_shape=jax.ShapeDtypeStruct((rows, width), bf16),
        in_specs=[vmem, pl.BlockSpec(memory_space=pl.ANY)],
        out_specs=vmem,
        scratch_shapes=[
            pltpu.VMEM((2, rows // 2, chans), bf16),
            pltpu.VMEM(w_out.shape, bf16),
            pltpu.VMEM((2, chips, rows // 2, width), jnp.float32),
            slots(chips),
            slots(chips),
            slots(chips - 1),
            slots(chips - 1),
            dma((2 * (seq_count - 1),)),
            dma((2 * (seq_count - 1),)),
            dma((2 * chips,)),
            dma((2 * chips,)),
            dma((2 * (chips - 1),)),
            dma((2 * (chips - 1),)),
            dma(()),
        ],
        compiler_params=pltpu.CompilerParams(
            collective_id=1, has_side_effects=True, vmem_limit_bytes=32 * 2**20
        ),
    )(folded, w_out)


def body(tokens, w_in, short_filter, mr_filter, skip_gain, w_out, segments):
    rows, width = tokens.shape
    seq_count = lax.axis_size("seq")
    taps = mr_filter.shape[1]
    fold = fold_matrix(rows, seq_count)
    chan_size = lax.axis_size("chan")
    if rows // seq_count % (2 * PACK) == 0 and chan_size % 2 == 0 and chan_size > 2:
        q, k, v, *halos = project(tokens, w_in, fold_matrix(rows // 2, seq_count).T, taps, seq_count, chan_size)
        folded = mix((q, k, v), halos, short_filter, mr_filter, skip_gain, segments, fold)
        return project_out(folded, w_out, seq_count, chan_size)
    pieces = tokens.reshape(seq_count, rows // seq_count, width)
    received = lax.all_to_all(pieces, "seq", split_axis=0, concat_axis=0, tiled=True)
    ordered = lax.dot_general(
        fold,
        received.reshape(rows, width),
        (((0,), (0,)), ((), ())),
        preferred_element_type=jnp.float32,
    ).astype(jnp.bfloat16)
    gathered = lax.all_gather(ordered, "chan", axis=1, tiled=True)
    q, k, v = [
        jnp.dot(gathered, w_in[:, i], preferred_element_type=jnp.float32).astype(jnp.bfloat16)
        for i in range(3)
    ]
    tails = (q[rows - PACK :], k[rows - taps - PACK :], v[rows - taps - PACK :])
    ring = [(i, i + 1) for i in range(seq_count - 1)]
    halos = lax.ppermute(tails, "seq", ring)
    folded = mix((q, k, v), halos, short_filter, mr_filter, skip_gain, segments, fold)
    outgoing = folded.reshape(seq_count, rows // seq_count, folded.shape[1])
    returned = lax.all_to_all(outgoing, "seq", split_axis=0, concat_axis=0, tiled=True)
    partial = jnp.dot(
        returned.reshape(rows, -1), w_out, preferred_element_type=jnp.float32
    ).astype(jnp.bfloat16)
    return lax.psum_scatter(partial, "chan", scatter_dimension=1, tiled=True)


def solution(mesh):
    return jax.shard_map(
        body,
        mesh=mesh,
        in_specs=(
            P("seq", "chan"),
            P(None, None, "chan"),
            P(None, None, "chan"),
            P("chan", None),
            P("chan"),
            P("chan", None),
            P(),
        ),
        out_specs=P("seq", "chan"),
        check_vma=False,
    )
```

```python
import functools

import jax
import jax.numpy as jnp
from jax import lax
from jax.experimental import pallas as pl
from jax.experimental.pallas import tpu as pltpu
from jax.sharding import PartitionSpec as P

LANES = 128
PACK = 16


def fold_matrix(row_count, seq_count):
    periods = row_count // (2 * seq_count)
    out_row = lax.broadcasted_iota(jnp.int32, (row_count, row_count), 0)
    in_row = lax.broadcasted_iota(jnp.int32, (row_count, row_count), 1)
    d = out_row // (2 * periods)
    a = (out_row // 2) % periods
    s = out_row % 2
    wanted = a * 2 * seq_count + jnp.where(s == 0, d, 2 * seq_count - 1 - d)
    return (wanted == in_row).astype(jnp.bfloat16)


def short_conv(x, weights, masks, start):
    rows = x.shape[0] - start
    total = weights[0:1] * x[start:]
    for j in range(1, weights.shape[0]):
        total = total + weights[j : j + 1] * x[start - j : start - j + rows] * masks[:, j : j + 1]
    return total


def mix_kernel(
    gsize, q, k, v, hq, hk, hv, short, pattern, skip, near, seg_col, seg_row, fold, out
):
    rows, lanes = q.shape
    taps = pattern.shape[1] // 2
    groups = lanes // gsize
    f32 = jnp.float32
    masks = near[...]
    qx = jnp.concatenate([hq[...].astype(f32), q[...].astype(f32)])
    kx = jnp.concatenate([hk[...].astype(f32), k[...].astype(f32)])
    vx = jnp.concatenate([hv[...].astype(f32), v[...].astype(f32)])
    sq = short_conv(qx, short[:, 0], masks[taps:], hq.shape[0])
    sk = short_conv(kx, short[:, 1], masks, hk.shape[0] - taps)
    sv = short_conv(vx, short[:, 2], masks, hk.shape[0] - taps)
    gated = (sk * sv).astype(jnp.bfloat16)
    lane_group = lax.broadcasted_iota(jnp.int32, (taps, lanes), 1) // gsize
    bands = []
    for g in range(groups):
        row = jnp.broadcast_to(pattern[g : g + 1], (taps, 2 * taps))
        bands.append(pltpu.roll(row, 0, 1, stride=1, stride_axis=0))
    parts = []
    for b in range(rows // taps):
        same = seg_col[b * taps : (b + 1) * taps] == seg_row[:, b * taps : (b + 2) * taps]
        lhs = jnp.concatenate(
            [jnp.where(same, band, 0.0).astype(jnp.bfloat16) for band in bands]
        )
        window = gated[b * taps : (b + 2) * taps]
        every = jnp.dot(lhs, window, preferred_element_type=f32)
        total = jnp.zeros((taps, lanes), f32)
        for g in range(groups):
            total = jnp.where(lane_group == g, every[g * taps : (g + 1) * taps], total)
        parts.append(total)
    long_out = jnp.concatenate(parts)
    mixed = (sq * (long_out + skip[...] * gated[taps:].astype(f32))).astype(jnp.bfloat16)
    out[...] = jnp.dot(fold[...], mixed, preferred_element_type=f32).astype(jnp.bfloat16)


def mix(qkv, halos, short_filter, mr_filter, skip_gain, segments, fold):
    rows, chans = qkv[0].shape
    groups, taps = mr_filter.shape
    short_taps = short_filter.shape[0]
    gsize = chans // groups
    per = LANES // gsize
    base = lax.axis_index("seq") * rows
    lead = halos[1].shape[0]
    padded = jnp.concatenate([jnp.full((lead,), -1, jnp.int32), segments])
    ext = lax.dynamic_slice_in_dim(padded, base, rows + lead, 0)
    window = ext[lead - taps :]
    near = jnp.stack(
        [
            (ext[lead - taps - j : rows + lead - j] == window).astype(jnp.float32)
            for j in range(short_taps)
        ],
        axis=1,
    )
    pattern = jnp.pad(mr_filter[:, ::-1].astype(jnp.float32), ((0, 0), (1, taps - 1)))
    whole = lambda shape: pl.BlockSpec(shape, lambda i: (0, 0))
    lane = lambda height: pl.BlockSpec((height, LANES), lambda i: (0, i))
    return pl.pallas_call(
        functools.partial(mix_kernel, gsize),
        grid=(chans // LANES,),
        out_shape=jax.ShapeDtypeStruct((rows, chans), jnp.bfloat16),
        in_specs=[lane(rows)] * 3
        + [lane(h.shape[0]) for h in halos]
        + [
            pl.BlockSpec((short_taps, 3, LANES), lambda i: (0, 0, i)),
            pl.BlockSpec((per, 2 * taps), lambda i: (i, 0)),
            lane(1),
            whole(near.shape),
            whole((rows, 1)),
            whole((1, rows + taps)),
            whole(fold.shape),
        ],
        out_specs=lane(rows),
        compiler_params=pltpu.CompilerParams(vmem_limit_bytes=32 * 2**20),
    )(
        *qkv,
        *halos,
        short_filter,
        pattern,
        skip_gain[None],
        near,
        ext[lead:, None],
        window[None],
        fold,
    )


def remote(src, dst, sems, index, device):
    send, recv = sems
    return pltpu.make_async_remote_copy(
        src_ref=src,
        dst_ref=dst,
        send_sem=send.at[index],
        recv_sem=recv.at[index],
        device_id=device,
        device_id_type=pl.DeviceIdType.MESH,
    )


def place(seq_count, chan_count):
    chan = lax.axis_index("chan")
    return lax.axis_index("seq"), chan // 2, chan % 2, chan_count // 2


def greet(devices):
    barrier = pltpu.get_barrier_semaphore()
    for device in devices:
        pl.semaphore_signal(
            barrier, inc=1, device_id=device, device_id_type=pl.DeviceIdType.MESH
        )
    pl.semaphore_wait(barrier, len(devices))


def partners(seq, chip, core, seq_count, chips):
    rows = [{"seq": lax.rem(seq + o, seq_count)} for o in range(1, seq_count)]
    across = [{"chan": lax.rem(chip + o, chips) * 2 + core} for o in range(1, chips)]
    return rows, across, {"chan": chip * 2 + 1 - core}


HALVES = (1, 0)


def exchange_rows(source, target, sems, seq, devices, half):
    count = len(devices) + 1
    piece = source.shape[0] // count
    part = piece // 2
    take = lambda d: source.at[pl.ds(pl.multiple_of(d * piece + half * part, part), part)]
    put = target.at[half, pl.ds(pl.multiple_of(seq * part, part), part)]
    copies = []
    for o in range(1, count):
        index = half * (count - 1) + o - 1
        copies.append(remote(take(lax.rem(seq + o, count)), put, sems, index, devices[o - 1]))
        copies[-1].start()
    put[...] = take(seq)[...]
    return copies


def project_kernel(
    seq_count, chan_count, tokens, w, order, q, k, v, hq, hk, hv,
    landed, blocks, wbuf, total, row_send, row_recv, col_send, col_recv, halo_send, halo_recv, w_sem,
):
    seq, chip, core, chips = place(seq_count, chan_count)
    rows_to, across, sibling = partners(seq, chip, core, seq_count, chips)
    rows, width = tokens.shape
    half_rows = rows // 2
    f32 = jnp.float32
    tile = min(256, wbuf.shape[2])
    tiles = wbuf.shape[2] // tile

    uses = [chip * 2 + core, chip * 2 + 1 - core]
    for o in range(1, chips):
        origin = lax.rem(chip - o + chips, chips)
        uses += [origin * 2 + core, origin * 2 + 1 - core]
    part = lambda c: pl.ds(pl.multiple_of(c * width, width), width)
    loads = []
    for n, c in enumerate(uses):
        loads.append(
            pltpu.make_async_copy(w.at[:, part(c)], wbuf.at[:, part(c)], w_sem.at[n])
        )
        loads[-1].start()

    greet(rows_to + across + [sibling])
    row_sems = (row_send, row_recv)
    copies = {h: exchange_rows(tokens, landed, row_sems, seq, rows_to, h) for h in HALVES}
    mine = uses[0]
    sems = (col_send, col_recv)
    outs, inner = {}, {}

    block = lambda c, h: blocks.at[c, pl.ds(h * half_rows, half_rows)]

    def spread(h):
        for copy in copies[h]:
            copy.wait()
        own = block(mine, h)
        own[...] = jnp.dot(order[...], landed[h], preferred_element_type=f32).astype(jnp.bfloat16)
        first = h * (chan_count - 1)
        outs[h] = [remote(own, own, sems, first + o, across[o - 1]) for o in range(1, chips)]
        inner[h] = remote(own, own, sems, first, sibling)
        for copy in outs[h] + [inner[h]]:
            copy.start()

    def multiply(n, i, target=None):
        c = uses[n]

        @pl.loop(0, tiles)
        def _(t):
            cols = pl.ds(pl.multiple_of(t * tile, tile), tile)
            term = jnp.dot(blocks[c], wbuf[i, part(c), cols], preferred_element_type=f32)
            if n > 0:
                term += total[i, :, cols]
            if target is None:
                total[i, :, cols] = term
            else:
                target[:, cols] = term.astype(jnp.bfloat16)

    def forward(o):
        copies = []
        for h in HALVES:
            outs[h][o - 1].wait_recv()
            ref = block(uses[2 * o], h)
            index = h * (chan_count - 1) + chips - 1 + o
            copies.append(remote(ref, ref, sems, index, sibling))
            copies[-1].start()
        return copies

    for h in HALVES:
        spread(h)
    last = chan_count - 1
    forwards = []
    halos = []
    for n in range(chan_count):
        loads[n].wait()
        if n == 1:
            for h in HALVES:
                inner[h].wait_recv()
        elif n > 1 and n % 2 == 0:
            forwards = forward(n // 2)
        elif n > 1:
            for copy in forwards:
                copy.wait()
        if n < last:
            for i in range(3):
                multiply(n, i)
    for i, ref, halo in ((1, k, hk), (2, v, hv), (0, q, hq)):
        multiply(last, i, ref)
        tail = halo.shape[0]
        src = ref.at[pl.ds(rows - tail, tail)]
        halos.append(remote(src, halo, (halo_send, halo_recv), i, rows_to[0]))
        halos[-1].start()
    for h in HALVES:
        for copy in outs[h] + [inner[h]]:
            copy.wait_send()
    for copy in halos:
        copy.wait()


def project(tokens, w_in, order, taps, seq_count, chan_count):
    rows, width = tokens.shape
    chans = w_in.shape[2]
    vmem = pl.BlockSpec(memory_space=pltpu.VMEM)
    bf16 = jnp.bfloat16
    dma = pltpu.SemaphoreType.DMA
    shape = lambda height: jax.ShapeDtypeStruct((height, chans), bf16)
    return pl.pallas_call(
        functools.partial(project_kernel, seq_count, chan_count),
        out_shape=[shape(rows)] * 3 + [shape(PACK)] + [shape(taps + PACK)] * 2,
        in_specs=[vmem, pl.BlockSpec(memory_space=pl.ANY), vmem],
        out_specs=[vmem] * 6,
        scratch_shapes=[
            pltpu.VMEM((2, rows // 2, width), bf16),
            pltpu.VMEM((chan_count, rows, width), bf16),
            pltpu.VMEM((3, w_in.shape[0], chans), bf16),
            pltpu.VMEM((3, rows, chans), jnp.float32),
            dma((2 * (seq_count - 1),)),
            dma((2 * (seq_count - 1),)),
            dma((2 * (chan_count - 1),)),
            dma((2 * (chan_count - 1),)),
            dma((3,)),
            dma((3,)),
            dma((chan_count,)),
        ],
        compiler_params=pltpu.CompilerParams(
            collective_id=0, has_side_effects=True, vmem_limit_bytes=48 * 2**20
        ),
    )(tokens, jnp.swapaxes(w_in, 0, 1), order)


def output_kernel(
    seq_count, chan_count, folded, w, out,
    landed, wbuf, kept, inner_out, inner_in, across_out, across_in,
    row_send, row_recv, inner_send, inner_recv, across_send, across_recv, w_sem,
):
    seq, chip, core, chips = place(seq_count, chan_count)
    rows_to, across, sibling = partners(seq, chip, core, seq_count, chips)
    f32 = jnp.float32
    width = out.shape[1]
    tile = min(256, width)
    load = pltpu.make_async_copy(w, wbuf, w_sem)
    load.start()
    greet(rows_to + across + [sibling])
    row_sems = (row_send, row_recv)
    copies = {h: exchange_rows(folded, landed, row_sems, seq, rows_to, h) for h in HALVES}

    half_rows = landed.shape[1]

    def multiply(halves, c, target, slot):
        @pl.loop(0, width // tile)
        def _(t):
            start = pl.multiple_of(t * tile, tile)
            cols = pl.ds(pl.multiple_of(c * width + start, tile), tile)
            lhs = jnp.concatenate([landed[h] for h in halves])
            term = jnp.dot(lhs, wbuf[:, cols], preferred_element_type=f32).astype(target.dtype)
            for n, h in enumerate(halves):
                rows = term[n * half_rows : (n + 1) * half_rows]
                target[h, slot, :, pl.ds(start, tile)] = rows

    inners, outs = {0: [], 1: []}, {0: [], 1: []}

    def share(halves, c, slot):
        multiply(halves, c * 2 + 1 - core, inner_out, slot)
        for h in halves:
            src, dst = inner_out.at[h, slot], inner_in.at[h, slot]
            index = h * chips + slot
            inners[h].append(remote(src, dst, (inner_send, inner_recv), index, sibling))
            inners[h][-1].start()
        multiply(halves, c * 2 + core, kept, slot)

    for h in HALVES:
        for copy in copies[h]:
            copy.wait()
        if h == HALVES[0]:
            load.wait()
        for o in range(1, chips):
            n = o - 1
            share((h,), lax.rem(chip + o, chips), n)
            inners[h][-1].wait_recv()
            across_out[h, n] = (kept[h, n] + inner_in[h, n].astype(f32)).astype(jnp.bfloat16)
            src, dst = across_out.at[h, n], across_in.at[h, n]
            index = h * (chips - 1) + n
            outs[h].append(remote(src, dst, (across_send, across_recv), index, across[n]))
            outs[h][-1].start()
    share(HALVES, chip, chips - 1)

    part = landed.shape[1] // seq_count
    for h in HALVES:
        inners[h][-1].wait_recv()
        result = kept[h, chips - 1] + inner_in[h, chips - 1].astype(f32)
        for o in range(1, chips):
            outs[h][o - 1].wait_recv()
            result = result + across_in[h, o - 1].astype(f32)
        result = result.astype(out.dtype)
        for d in range(seq_count):
            out[pl.ds((2 * d + h) * part, part)] = result[d * part : (d + 1) * part]
    for h in HALVES:
        for copy in inners[h] + outs[h]:
            copy.wait_send()


def project_out(folded, w_out, seq_count, chan_count):
    rows, chans = folded.shape
    width = w_out.shape[1] // chan_count
    chips = chan_count // 2
    vmem = pl.BlockSpec(memory_space=pltpu.VMEM)
    bf16 = jnp.bfloat16
    dma = pltpu.SemaphoreType.DMA
    slots = lambda count: pltpu.VMEM((2, count, rows // 2, width), bf16)
    return pl.pallas_call(
        functools.partial(output_kernel, seq_count, chan_count),
        out_shape=jax.ShapeDtypeStruct((rows, width), bf16),
        in_specs=[vmem, pl.BlockSpec(memory_space=pl.ANY)],
        out_specs=vmem,
        scratch_shapes=[
            pltpu.VMEM((2, rows // 2, chans), bf16),
            pltpu.VMEM(w_out.shape, bf16),
            pltpu.VMEM((2, chips, rows // 2, width), jnp.float32),
            slots(chips),
            slots(chips),
            slots(chips - 1),
            slots(chips - 1),
            dma((2 * (seq_count - 1),)),
            dma((2 * (seq_count - 1),)),
            dma((2 * chips,)),
            dma((2 * chips,)),
            dma((2 * (chips - 1),)),
            dma((2 * (chips - 1),)),
            dma(()),
        ],
        compiler_params=pltpu.CompilerParams(
            collective_id=1, has_side_effects=True, vmem_limit_bytes=32 * 2**20
        ),
    )(folded, w_out)


def body(tokens, w_in, short_filter, mr_filter, skip_gain, w_out, segments):
    rows, width = tokens.shape
    seq_count = lax.axis_size("seq")
    taps = mr_filter.shape[1]
    fold = fold_matrix(rows, seq_count)
    chan_size = lax.axis_size("chan")
    if rows // seq_count % (2 * PACK) == 0 and chan_size % 2 == 0 and chan_size > 2:
        q, k, v, *halos = project(tokens, w_in, fold_matrix(rows // 2, seq_count).T, taps, seq_count, chan_size)
        folded = mix((q, k, v), halos, short_filter, mr_filter, skip_gain, segments, fold)
        return project_out(folded, w_out, seq_count, chan_size)
    pieces = tokens.reshape(seq_count, rows // seq_count, width)
    received = lax.all_to_all(pieces, "seq", split_axis=0, concat_axis=0, tiled=True)
    ordered = lax.dot_general(
        fold,
        received.reshape(rows, width),
        (((0,), (0,)), ((), ())),
        preferred_element_type=jnp.float32,
    ).astype(jnp.bfloat16)
    gathered = lax.all_gather(ordered, "chan", axis=1, tiled=True)
    q, k, v = [
        jnp.dot(gathered, w_in[:, i], preferred_element_type=jnp.float32).astype(jnp.bfloat16)
        for i in range(3)
    ]
    tails = (q[rows - PACK :], k[rows - taps - PACK :], v[rows - taps - PACK :])
    ring = [(i, i + 1) for i in range(seq_count - 1)]
    halos = lax.ppermute(tails, "seq", ring)
    folded = mix((q, k, v), halos, short_filter, mr_filter, skip_gain, segments, fold)
    outgoing = folded.reshape(seq_count, rows // seq_count, folded.shape[1])
    returned = lax.all_to_all(outgoing, "seq", split_axis=0, concat_axis=0, tiled=True)
    partial = jnp.dot(
        returned.reshape(rows, -1), w_out, preferred_element_type=jnp.float32
    ).astype(jnp.bfloat16)
    return lax.psum_scatter(partial, "chan", scatter_dimension=1, tiled=True)


def solution(mesh):
    return jax.shard_map(
        body,
        mesh=mesh,
        in_specs=(
            P("seq", "chan"),
            P(None, None, "chan"),
            P(None, None, "chan"),
            P("chan", None),
            P("chan"),
            P("chan", None),
            P(),
        ),
        out_specs=P("seq", "chan"),
        check_vma=False,
    )
```

```python
import functools

import jax
import jax.numpy as jnp
from jax import lax
from jax.experimental import pallas as pl
from jax.experimental.pallas import tpu as pltpu
from jax.sharding import PartitionSpec as P

LANES = 128
PACK = 16


def fold_matrix(row_count, seq_count):
    periods = row_count // (2 * seq_count)
    out_row = lax.broadcasted_iota(jnp.int32, (row_count, row_count), 0)
    in_row = lax.broadcasted_iota(jnp.int32, (row_count, row_count), 1)
    d = out_row // (2 * periods)
    a = (out_row // 2) % periods
    s = out_row % 2
    wanted = a * 2 * seq_count + jnp.where(s == 0, d, 2 * seq_count - 1 - d)
    return (wanted == in_row).astype(jnp.bfloat16)


def short_conv(x, weights, masks, start):
    rows = x.shape[0] - start
    total = weights[0:1] * x[start:]
    for j in range(1, weights.shape[0]):
        total = total + weights[j : j + 1] * x[start - j : start - j + rows] * masks[:, j : j + 1]
    return total


def mix_kernel(
    gsize, q, k, v, hq, hk, hv, short, pattern, skip, near, seg_col, seg_row, fold, out
):
    rows, lanes = q.shape
    taps = pattern.shape[1] // 2
    groups = lanes // gsize
    f32 = jnp.float32
    masks = near[...]
    qx = jnp.concatenate([hq[...].astype(f32), q[...].astype(f32)])
    kx = jnp.concatenate([hk[...].astype(f32), k[...].astype(f32)])
    vx = jnp.concatenate([hv[...].astype(f32), v[...].astype(f32)])
    sq = short_conv(qx, short[:, 0], masks[taps:], hq.shape[0])
    sk = short_conv(kx, short[:, 1], masks, hk.shape[0] - taps)
    sv = short_conv(vx, short[:, 2], masks, hk.shape[0] - taps)
    gated = (sk * sv).astype(jnp.bfloat16)
    lane_group = lax.broadcasted_iota(jnp.int32, (taps, lanes), 1) // gsize
    bands = []
    for g in range(groups):
        row = jnp.broadcast_to(pattern[g : g + 1], (taps, 2 * taps))
        bands.append(pltpu.roll(row, 0, 1, stride=1, stride_axis=0))
    parts = []
    for b in range(rows // taps):
        same = seg_col[b * taps : (b + 1) * taps] == seg_row[:, b * taps : (b + 2) * taps]
        lhs = jnp.concatenate(
            [jnp.where(same, band, 0.0).astype(jnp.bfloat16) for band in bands]
        )
        window = gated[b * taps : (b + 2) * taps]
        every = jnp.dot(lhs, window, preferred_element_type=f32)
        total = jnp.zeros((taps, lanes), f32)
        for g in range(groups):
            total = jnp.where(lane_group == g, every[g * taps : (g + 1) * taps], total)
        parts.append(total)
    long_out = jnp.concatenate(parts)
    mixed = (sq * (long_out + skip[...] * gated[taps:].astype(f32))).astype(jnp.bfloat16)
    out[...] = jnp.dot(fold[...], mixed, preferred_element_type=f32).astype(jnp.bfloat16)


def mix(qkv, halos, short_filter, mr_filter, skip_gain, segments, fold):
    rows, chans = qkv[0].shape
    groups, taps = mr_filter.shape
    short_taps = short_filter.shape[0]
    gsize = chans // groups
    per = LANES // gsize
    base = lax.axis_index("seq") * rows
    lead = halos[1].shape[0]
    padded = jnp.concatenate([jnp.full((lead,), -1, jnp.int32), segments])
    ext = lax.dynamic_slice_in_dim(padded, base, rows + lead, 0)
    window = ext[lead - taps :]
    near = jnp.stack(
        [
            (ext[lead - taps - j : rows + lead - j] == window).astype(jnp.float32)
            for j in range(short_taps)
        ],
        axis=1,
    )
    pattern = jnp.pad(mr_filter[:, ::-1].astype(jnp.float32), ((0, 0), (1, taps - 1)))
    whole = lambda shape: pl.BlockSpec(shape, lambda i: (0, 0))
    lane = lambda height: pl.BlockSpec((height, LANES), lambda i: (0, i))
    return pl.pallas_call(
        functools.partial(mix_kernel, gsize),
        grid=(chans // LANES,),
        out_shape=jax.ShapeDtypeStruct((rows, chans), jnp.bfloat16),
        in_specs=[lane(rows)] * 3
        + [lane(h.shape[0]) for h in halos]
        + [
            pl.BlockSpec((short_taps, 3, LANES), lambda i: (0, 0, i)),
            pl.BlockSpec((per, 2 * taps), lambda i: (i, 0)),
            lane(1),
            whole(near.shape),
            whole((rows, 1)),
            whole((1, rows + taps)),
            whole(fold.shape),
        ],
        out_specs=lane(rows),
        compiler_params=pltpu.CompilerParams(vmem_limit_bytes=32 * 2**20),
    )(
        *qkv,
        *halos,
        short_filter,
        pattern,
        skip_gain[None],
        near,
        ext[lead:, None],
        window[None],
        fold,
    )


def remote(src, dst, sems, index, device):
    send, recv = sems
    return pltpu.make_async_remote_copy(
        src_ref=src,
        dst_ref=dst,
        send_sem=send.at[index],
        recv_sem=recv.at[index],
        device_id=device,
        device_id_type=pl.DeviceIdType.MESH,
    )


def place(seq_count, chan_count):
    chan = lax.axis_index("chan")
    return lax.axis_index("seq"), chan // 2, chan % 2, chan_count // 2


def greet(devices):
    barrier = pltpu.get_barrier_semaphore()
    for device in devices:
        pl.semaphore_signal(
            barrier, inc=1, device_id=device, device_id_type=pl.DeviceIdType.MESH
        )
    pl.semaphore_wait(barrier, len(devices))


def partners(seq, chip, core, seq_count, chips):
    rows = [{"seq": lax.rem(seq + o, seq_count)} for o in range(1, seq_count)]
    across = [{"chan": lax.rem(chip + o, chips) * 2 + core} for o in range(1, chips)]
    return rows, across, {"chan": chip * 2 + 1 - core}


HALVES = (1, 0)


def exchange_rows(source, target, sems, seq, devices, half):
    count = len(devices) + 1
    piece = source.shape[0] // count
    part = piece // 2
    take = lambda d: source.at[pl.ds(pl.multiple_of(d * piece + half * part, part), part)]
    put = target.at[half, pl.ds(pl.multiple_of(seq * part, part), part)]
    copies = []
    for o in range(1, count):
        index = half * (count - 1) + o - 1
        copies.append(remote(take(lax.rem(seq + o, count)), put, sems, index, devices[o - 1]))
        copies[-1].start()
    put[...] = take(seq)[...]
    return copies


def project_kernel(
    seq_count, chan_count, tokens, w, order, q, k, v, hq, hk, hv,
    landed, blocks, wbuf, total, row_send, row_recv, col_send, col_recv, halo_send, halo_recv, w_sem,
):
    seq, chip, core, chips = place(seq_count, chan_count)
    rows_to, across, sibling = partners(seq, chip, core, seq_count, chips)
    rows, width = tokens.shape
    half_rows = rows // 2
    f32 = jnp.float32
    tile = min(256, wbuf.shape[2])
    tiles = wbuf.shape[2] // tile

    uses = [chip * 2 + core, chip * 2 + 1 - core]
    for o in range(1, chips):
        origin = lax.rem(chip - o + chips, chips)
        uses += [origin * 2 + core, origin * 2 + 1 - core]
    part = lambda c: pl.ds(pl.multiple_of(c * width, width), width)
    loads = []
    for n, c in enumerate(uses):
        loads.append(
            pltpu.make_async_copy(w.at[:, part(c)], wbuf.at[:, part(c)], w_sem.at[n])
        )
        loads[-1].start()

    greet(rows_to + across + [sibling])
    row_sems = (row_send, row_recv)
    copies = {h: exchange_rows(tokens, landed, row_sems, seq, rows_to, h) for h in HALVES}
    mine = uses[0]
    sems = (col_send, col_recv)
    outs, inner = {}, {}

    block = lambda c, h: blocks.at[c, pl.ds(h * half_rows, half_rows)]

    def spread(h):
        for copy in copies[h]:
            copy.wait()
        own = block(mine, h)
        own[...] = jnp.dot(order[...], landed[h], preferred_element_type=f32).astype(jnp.bfloat16)
        first = h * (chan_count - 1)
        outs[h] = [remote(own, own, sems, first + o, across[o - 1]) for o in range(1, chips)]
        inner[h] = remote(own, own, sems, first, sibling)
        for copy in outs[h] + [inner[h]]:
            copy.start()

    last = chan_count - 1

    def multiply(n, i, span, target):
        c = uses[n]

        @pl.loop(0, tiles)
        def _(t):
            cols = pl.ds(pl.multiple_of(t * tile, tile), tile)
            term = jnp.dot(blocks[c, span], wbuf[i, part(c), cols], preferred_element_type=f32)
            if n > 0:
                term += total[i, span, cols]
            if n < last:
                total[i, span, cols] = term
            else:
                target[span, cols] = term.astype(jnp.bfloat16)

    forwards = {}

    def arrive(h, n):
        if n == 1:
            inner[h].wait_recv()
        elif n > 1 and n % 2 == 0:
            outs[h][n // 2 - 1].wait_recv()
            ref = block(uses[n], h)
            index = h * (chan_count - 1) + chips - 1 + n // 2
            forwards[h, n] = remote(ref, ref, sems, index, sibling)
            forwards[h, n].start()
        elif n > 1:
            forwards[h, n - 1].wait()

    halos = []

    def send_halo(i, ref, halo, h):
        lead = rows - halo.shape[0]
        start = max(lead, h * half_rows)
        size = (h + 1) * half_rows - start
        if size > 0:
            src = ref.at[pl.ds(start, size)]
            dst = halo.at[pl.ds(start - lead, size)]
            halos.append(remote(src, dst, (halo_send, halo_recv), h * 3 + i, rows_to[0]))
            halos[-1].start()

    pair = ((1, k, hk), (2, v, hv))
    spread(1)
    for n in range(chan_count):
        loads[n].wait()
        arrive(1, n)
        for i, ref, halo in pair:
            multiply(n, i, pl.ds(half_rows, half_rows), ref)
            if n == last:
                send_halo(i, ref, halo, 1)
        if n == 0:
            spread(0)
    for n in range(chan_count):
        arrive(0, n)
        multiply(n, 0, pl.ds(0, rows), q)
    send_halo(0, q, hq, 1)
    for i, ref, halo in pair:
        for n in range(chan_count):
            multiply(n, i, pl.ds(0, half_rows), ref)
        send_halo(i, ref, halo, 0)
    for h in HALVES:
        for copy in outs[h] + [inner[h]]:
            copy.wait_send()
    for copy in halos:
        copy.wait()


def project(tokens, w_in, order, taps, seq_count, chan_count):
    rows, width = tokens.shape
    chans = w_in.shape[2]
    vmem = pl.BlockSpec(memory_space=pltpu.VMEM)
    bf16 = jnp.bfloat16
    dma = pltpu.SemaphoreType.DMA
    shape = lambda height: jax.ShapeDtypeStruct((height, chans), bf16)
    return pl.pallas_call(
        functools.partial(project_kernel, seq_count, chan_count),
        out_shape=[shape(rows)] * 3 + [shape(PACK)] + [shape(taps + PACK)] * 2,
        in_specs=[vmem, pl.BlockSpec(memory_space=pl.ANY), vmem],
        out_specs=[vmem] * 6,
        scratch_shapes=[
            pltpu.VMEM((2, rows // 2, width), bf16),
            pltpu.VMEM((chan_count, rows, width), bf16),
            pltpu.VMEM((3, w_in.shape[0], chans), bf16),
            pltpu.VMEM((3, rows, chans), jnp.float32),
            dma((2 * (seq_count - 1),)),
            dma((2 * (seq_count - 1),)),
            dma((2 * (chan_count - 1),)),
            dma((2 * (chan_count - 1),)),
            dma((6,)),
            dma((6,)),
            dma((chan_count,)),
        ],
        compiler_params=pltpu.CompilerParams(
            collective_id=0, has_side_effects=True, vmem_limit_bytes=48 * 2**20
        ),
    )(tokens, jnp.swapaxes(w_in, 0, 1), order)


def output_kernel(
    seq_count, chan_count, folded, w, out,
    landed, wbuf, kept, inner_out, inner_in, across_out, across_in,
    row_send, row_recv, inner_send, inner_recv, across_send, across_recv, w_sem,
):
    seq, chip, core, chips = place(seq_count, chan_count)
    rows_to, across, sibling = partners(seq, chip, core, seq_count, chips)
    f32 = jnp.float32
    width = out.shape[1]
    tile = min(256, width)
    load = pltpu.make_async_copy(w, wbuf, w_sem)
    load.start()
    greet(rows_to + across + [sibling])
    row_sems = (row_send, row_recv)
    copies = {h: exchange_rows(folded, landed, row_sems, seq, rows_to, h) for h in HALVES}

    half_rows = landed.shape[1]

    def multiply(halves, c, target, slot):
        @pl.loop(0, width // tile)
        def _(t):
            start = pl.multiple_of(t * tile, tile)
            cols = pl.ds(pl.multiple_of(c * width + start, tile), tile)
            lhs = jnp.concatenate([landed[h] for h in halves])
            term = jnp.dot(lhs, wbuf[:, cols], preferred_element_type=f32).astype(target.dtype)
            for n, h in enumerate(halves):
                rows = term[n * half_rows : (n + 1) * half_rows]
                target[h, slot, :, pl.ds(start, tile)] = rows

    inners, outs = {0: [], 1: []}, {0: [], 1: []}

    def share(halves, c, slot):
        multiply(halves, c * 2 + 1 - core, inner_out, slot)
        for h in halves:
            src, dst = inner_out.at[h, slot], inner_in.at[h, slot]
            index = h * chips + slot
            inners[h].append(remote(src, dst, (inner_send, inner_recv), index, sibling))
            inners[h][-1].start()
        multiply(halves, c * 2 + core, kept, slot)

    for h in HALVES:
        for copy in copies[h]:
            copy.wait()
        if h == HALVES[0]:
            load.wait()
        for o in range(1, chips):
            n = o - 1
            share((h,), lax.rem(chip + o, chips), n)
            inners[h][-1].wait_recv()
            across_out[h, n] = (kept[h, n] + inner_in[h, n].astype(f32)).astype(jnp.bfloat16)
            src, dst = across_out.at[h, n], across_in.at[h, n]
            index = h * (chips - 1) + n
            outs[h].append(remote(src, dst, (across_send, across_recv), index, across[n]))
            outs[h][-1].start()
    share(HALVES, chip, chips - 1)

    part = landed.shape[1] // seq_count
    for h in HALVES:
        inners[h][-1].wait_recv()
        result = kept[h, chips - 1] + inner_in[h, chips - 1].astype(f32)
        for o in range(1, chips):
            outs[h][o - 1].wait_recv()
            result = result + across_in[h, o - 1].astype(f32)
        result = result.astype(out.dtype)
        for d in range(seq_count):
            out[pl.ds((2 * d + h) * part, part)] = result[d * part : (d + 1) * part]
    for h in HALVES:
        for copy in inners[h] + outs[h]:
            copy.wait_send()


def project_out(folded, w_out, seq_count, chan_count):
    rows, chans = folded.shape
    width = w_out.shape[1] // chan_count
    chips = chan_count // 2
    vmem = pl.BlockSpec(memory_space=pltpu.VMEM)
    bf16 = jnp.bfloat16
    dma = pltpu.SemaphoreType.DMA
    slots = lambda count: pltpu.VMEM((2, count, rows // 2, width), bf16)
    return pl.pallas_call(
        functools.partial(output_kernel, seq_count, chan_count),
        out_shape=jax.ShapeDtypeStruct((rows, width), bf16),
        in_specs=[vmem, pl.BlockSpec(memory_space=pl.ANY)],
        out_specs=vmem,
        scratch_shapes=[
            pltpu.VMEM((2, rows // 2, chans), bf16),
            pltpu.VMEM(w_out.shape, bf16),
            pltpu.VMEM((2, chips, rows // 2, width), jnp.float32),
            slots(chips),
            slots(chips),
            slots(chips - 1),
            slots(chips - 1),
            dma((2 * (seq_count - 1),)),
            dma((2 * (seq_count - 1),)),
            dma((2 * chips,)),
            dma((2 * chips,)),
            dma((2 * (chips - 1),)),
            dma((2 * (chips - 1),)),
            dma(()),
        ],
        compiler_params=pltpu.CompilerParams(
            collective_id=1, has_side_effects=True, vmem_limit_bytes=32 * 2**20
        ),
    )(folded, w_out)


def body(tokens, w_in, short_filter, mr_filter, skip_gain, w_out, segments):
    rows, width = tokens.shape
    seq_count = lax.axis_size("seq")
    taps = mr_filter.shape[1]
    fold = fold_matrix(rows, seq_count)
    chan_size = lax.axis_size("chan")
    if rows // seq_count % (2 * PACK) == 0 and chan_size % 2 == 0 and chan_size > 2:
        q, k, v, *halos = project(tokens, w_in, fold_matrix(rows // 2, seq_count).T, taps, seq_count, chan_size)
        folded = mix((q, k, v), halos, short_filter, mr_filter, skip_gain, segments, fold)
        return project_out(folded, w_out, seq_count, chan_size)
    pieces = tokens.reshape(seq_count, rows // seq_count, width)
    received = lax.all_to_all(pieces, "seq", split_axis=0, concat_axis=0, tiled=True)
    ordered = lax.dot_general(
        fold,
        received.reshape(rows, width),
        (((0,), (0,)), ((), ())),
        preferred_element_type=jnp.float32,
    ).astype(jnp.bfloat16)
    gathered = lax.all_gather(ordered, "chan", axis=1, tiled=True)
    q, k, v = [
        jnp.dot(gathered, w_in[:, i], preferred_element_type=jnp.float32).astype(jnp.bfloat16)
        for i in range(3)
    ]
    tails = (q[rows - PACK :], k[rows - taps - PACK :], v[rows - taps - PACK :])
    ring = [(i, i + 1) for i in range(seq_count - 1)]
    halos = lax.ppermute(tails, "seq", ring)
    folded = mix((q, k, v), halos, short_filter, mr_filter, skip_gain, segments, fold)
    outgoing = folded.reshape(seq_count, rows // seq_count, folded.shape[1])
    returned = lax.all_to_all(outgoing, "seq", split_axis=0, concat_axis=0, tiled=True)
    partial = jnp.dot(
        returned.reshape(rows, -1), w_out, preferred_element_type=jnp.float32
    ).astype(jnp.bfloat16)
    return lax.psum_scatter(partial, "chan", scatter_dimension=1, tiled=True)


def solution(mesh):
    return jax.shard_map(
        body,
        mesh=mesh,
        in_specs=(
            P("seq", "chan"),
            P(None, None, "chan"),
            P(None, None, "chan"),
            P("chan", None),
            P("chan"),
            P("chan", None),
            P(),
        ),
        out_specs=P("seq", "chan"),
        check_vma=False,
    )
```

```python
import functools

import jax
import jax.numpy as jnp
from jax import lax
from jax.experimental import pallas as pl
from jax.experimental.pallas import tpu as pltpu
from jax.sharding import PartitionSpec as P

LANES = 128
PACK = 16


def fold_matrix(row_count, seq_count):
    periods = row_count // (2 * seq_count)
    out_row = lax.broadcasted_iota(jnp.int32, (row_count, row_count), 0)
    in_row = lax.broadcasted_iota(jnp.int32, (row_count, row_count), 1)
    d = out_row // (2 * periods)
    a = (out_row // 2) % periods
    s = out_row % 2
    wanted = a * 2 * seq_count + jnp.where(s == 0, d, 2 * seq_count - 1 - d)
    return (wanted == in_row).astype(jnp.bfloat16)


def short_conv(x, weights, masks, start):
    rows = x.shape[0] - start
    total = weights[0:1] * x[start:]
    for j in range(1, weights.shape[0]):
        total = total + weights[j : j + 1] * x[start - j : start - j + rows] * masks[:, j : j + 1]
    return total


def mix_kernel(
    gsize, q, k, v, hq, hk, hv, short, pattern, skip, near, seg_col, seg_row, fold, out
):
    rows, lanes = q.shape
    taps = pattern.shape[1] // 2
    groups = lanes // gsize
    f32 = jnp.float32
    masks = near[...]
    qx = jnp.concatenate([hq[...].astype(f32), q[...].astype(f32)])
    kx = jnp.concatenate([hk[...].astype(f32), k[...].astype(f32)])
    vx = jnp.concatenate([hv[...].astype(f32), v[...].astype(f32)])
    sq = short_conv(qx, short[:, 0], masks[taps:], hq.shape[0])
    sk = short_conv(kx, short[:, 1], masks, hk.shape[0] - taps)
    sv = short_conv(vx, short[:, 2], masks, hk.shape[0] - taps)
    gated = (sk * sv).astype(jnp.bfloat16)
    lane_group = lax.broadcasted_iota(jnp.int32, (taps, lanes), 1) // gsize
    bands = []
    for g in range(groups):
        row = jnp.broadcast_to(pattern[g : g + 1], (taps, 2 * taps))
        bands.append(pltpu.roll(row, 0, 1, stride=1, stride_axis=0))
    parts = []
    for b in range(rows // taps):
        same = seg_col[b * taps : (b + 1) * taps] == seg_row[:, b * taps : (b + 2) * taps]
        lhs = jnp.concatenate(
            [jnp.where(same, band, 0.0).astype(jnp.bfloat16) for band in bands]
        )
        window = gated[b * taps : (b + 2) * taps]
        every = jnp.dot(lhs, window, preferred_element_type=f32)
        total = jnp.zeros((taps, lanes), f32)
        for g in range(groups):
            total = jnp.where(lane_group == g, every[g * taps : (g + 1) * taps], total)
        parts.append(total)
    long_out = jnp.concatenate(parts)
    mixed = (sq * (long_out + skip[...] * gated[taps:].astype(f32))).astype(jnp.bfloat16)
    out[...] = jnp.dot(fold[...], mixed, preferred_element_type=f32).astype(jnp.bfloat16)


def mix(qkv, halos, short_filter, mr_filter, skip_gain, segments, fold):
    rows, chans = qkv[0].shape
    groups, taps = mr_filter.shape
    short_taps = short_filter.shape[0]
    gsize = chans // groups
    per = LANES // gsize
    base = lax.axis_index("seq") * rows
    lead = halos[1].shape[0]
    padded = jnp.concatenate([jnp.full((lead,), -1, jnp.int32), segments])
    ext = lax.dynamic_slice_in_dim(padded, base, rows + lead, 0)
    window = ext[lead - taps :]
    near = jnp.stack(
        [
            (ext[lead - taps - j : rows + lead - j] == window).astype(jnp.float32)
            for j in range(short_taps)
        ],
        axis=1,
    )
    pattern = jnp.pad(mr_filter[:, ::-1].astype(jnp.float32), ((0, 0), (1, taps - 1)))
    whole = lambda shape: pl.BlockSpec(shape, lambda i: (0, 0))
    lane = lambda height: pl.BlockSpec((height, LANES), lambda i: (0, i))
    return pl.pallas_call(
        functools.partial(mix_kernel, gsize),
        grid=(chans // LANES,),
        out_shape=jax.ShapeDtypeStruct((rows, chans), jnp.bfloat16),
        in_specs=[lane(rows)] * 3
        + [lane(h.shape[0]) for h in halos]
        + [
            pl.BlockSpec((short_taps, 3, LANES), lambda i: (0, 0, i)),
            pl.BlockSpec((per, 2 * taps), lambda i: (i, 0)),
            lane(1),
            whole(near.shape),
            whole((rows, 1)),
            whole((1, rows + taps)),
            whole(fold.shape),
        ],
        out_specs=lane(rows),
        compiler_params=pltpu.CompilerParams(vmem_limit_bytes=32 * 2**20),
    )(
        *qkv,
        *halos,
        short_filter,
        pattern,
        skip_gain[None],
        near,
        ext[lead:, None],
        window[None],
        fold,
    )


def remote(src, dst, sems, index, device):
    send, recv = sems
    return pltpu.make_async_remote_copy(
        src_ref=src,
        dst_ref=dst,
        send_sem=send.at[index],
        recv_sem=recv.at[index],
        device_id=device,
        device_id_type=pl.DeviceIdType.MESH,
    )


def place(seq_count, chan_count):
    chan = lax.axis_index("chan")
    return lax.axis_index("seq"), chan // 2, chan % 2, chan_count // 2


def greet(devices):
    barrier = pltpu.get_barrier_semaphore()
    for device in devices:
        pl.semaphore_signal(
            barrier, inc=1, device_id=device, device_id_type=pl.DeviceIdType.MESH
        )
    pl.semaphore_wait(barrier, len(devices))


def partners(seq, chip, core, seq_count, chips):
    rows = [{"seq": lax.rem(seq + o, seq_count)} for o in range(1, seq_count)]
    across = [{"chan": lax.rem(chip + o, chips) * 2 + core} for o in range(1, chips)]
    return rows, across, {"chan": chip * 2 + 1 - core}


HALVES = (1, 0)


def exchange_rows(source, target, sems, seq, devices, half):
    count = len(devices) + 1
    piece = source.shape[0] // count
    part = piece // 2
    take = lambda d: source.at[pl.ds(pl.multiple_of(d * piece + half * part, part), part)]
    put = target.at[half, pl.ds(pl.multiple_of(seq * part, part), part)]
    copies = []
    for o in range(1, count):
        index = half * (count - 1) + o - 1
        copies.append(remote(take(lax.rem(seq + o, count)), put, sems, index, devices[o - 1]))
        copies[-1].start()
    put[...] = take(seq)[...]
    return copies


def project_kernel(
    seq_count, chan_count, tokens, w, order, q, k, v, hq, hk, hv,
    landed, blocks, wbuf, total, row_send, row_recv, col_send, col_recv, halo_send, halo_recv, w_sem,
):
    seq, chip, core, chips = place(seq_count, chan_count)
    rows_to, across, sibling = partners(seq, chip, core, seq_count, chips)
    rows, width = tokens.shape
    half_rows = rows // 2
    f32 = jnp.float32
    tile = min(512, wbuf.shape[2])
    tiles = wbuf.shape[2] // tile

    uses = [chip * 2 + core, chip * 2 + 1 - core]
    for o in range(1, chips):
        origin = lax.rem(chip - o + chips, chips)
        uses += [origin * 2 + core, origin * 2 + 1 - core]
    part = lambda c: pl.ds(pl.multiple_of(c * width, width), width)
    loads = []
    for n, c in enumerate(uses):
        loads.append(
            pltpu.make_async_copy(w.at[:, part(c)], wbuf.at[:, part(c)], w_sem.at[n])
        )
        loads[-1].start()

    greet(rows_to + across + [sibling])
    row_sems = (row_send, row_recv)
    copies = {h: exchange_rows(tokens, landed, row_sems, seq, rows_to, h) for h in HALVES}
    mine = uses[0]
    sems = (col_send, col_recv)
    outs, inner = {}, {}

    block = lambda c, h: blocks.at[c, pl.ds(h * half_rows, half_rows)]

    def spread(h):
        for copy in copies[h]:
            copy.wait()
        own = block(mine, h)
        own[...] = jnp.dot(order[...], landed[h], preferred_element_type=f32).astype(jnp.bfloat16)
        first = h * (chan_count - 1)
        outs[h] = [remote(own, own, sems, first + o, across[o - 1]) for o in range(1, chips)]
        inner[h] = remote(own, own, sems, first, sibling)
        for copy in outs[h] + [inner[h]]:
            copy.start()

    last = chan_count - 1

    def multiply(n, i, span, target):
        c = uses[n]

        @pl.loop(0, tiles)
        def _(t):
            cols = pl.ds(pl.multiple_of(t * tile, tile), tile)
            term = jnp.dot(blocks[c, span], wbuf[i, part(c), cols], preferred_element_type=f32)
            if n > 0:
                term += total[i, span, cols]
            if n < last:
                total[i, span, cols] = term
            else:
                target[span, cols] = term.astype(jnp.bfloat16)

    forwards = {}

    def arrive(h, n):
        if n == 1:
            inner[h].wait_recv()
        elif n > 1 and n % 2 == 0:
            outs[h][n // 2 - 1].wait_recv()
            ref = block(uses[n], h)
            index = h * (chan_count - 1) + chips - 1 + n // 2
            forwards[h, n] = remote(ref, ref, sems, index, sibling)
            forwards[h, n].start()
        elif n > 1:
            forwards[h, n - 1].wait()

    halos = []

    def send_halo(i, ref, halo, h):
        lead = rows - halo.shape[0]
        start = max(lead, h * half_rows)
        size = (h + 1) * half_rows - start
        if size > 0:
            src = ref.at[pl.ds(start, size)]
            dst = halo.at[pl.ds(start - lead, size)]
            halos.append(remote(src, dst, (halo_send, halo_recv), h * 3 + i, rows_to[0]))
            halos[-1].start()

    pair = ((1, k, hk), (2, v, hv))
    spread(1)
    for n in range(chan_count):
        loads[n].wait()
        arrive(1, n)
        for i, ref, halo in pair:
            multiply(n, i, pl.ds(half_rows, half_rows), ref)
            if n == last:
                send_halo(i, ref, halo, 1)
        if n == 0:
            spread(0)
    for n in range(chan_count):
        arrive(0, n)
        multiply(n, 0, pl.ds(0, rows), q)
    send_halo(0, q, hq, 1)
    for i, ref, halo in pair:
        for n in range(chan_count):
            multiply(n, i, pl.ds(0, half_rows), ref)
        send_halo(i, ref, halo, 0)
    for h in HALVES:
        for copy in outs[h] + [inner[h]]:
            copy.wait_send()
    for copy in halos:
        copy.wait()


def project(tokens, w_in, order, taps, seq_count, chan_count):
    rows, width = tokens.shape
    chans = w_in.shape[2]
    vmem = pl.BlockSpec(memory_space=pltpu.VMEM)
    bf16 = jnp.bfloat16
    dma = pltpu.SemaphoreType.DMA
    shape = lambda height: jax.ShapeDtypeStruct((height, chans), bf16)
    return pl.pallas_call(
        functools.partial(project_kernel, seq_count, chan_count),
        out_shape=[shape(rows)] * 3 + [shape(PACK)] + [shape(taps + PACK)] * 2,
        in_specs=[vmem, pl.BlockSpec(memory_space=pl.ANY), vmem],
        out_specs=[vmem] * 6,
        scratch_shapes=[
            pltpu.VMEM((2, rows // 2, width), bf16),
            pltpu.VMEM((chan_count, rows, width), bf16),
            pltpu.VMEM((3, w_in.shape[0], chans), bf16),
            pltpu.VMEM((3, rows, chans), jnp.float32),
            dma((2 * (seq_count - 1),)),
            dma((2 * (seq_count - 1),)),
            dma((2 * (chan_count - 1),)),
            dma((2 * (chan_count - 1),)),
            dma((6,)),
            dma((6,)),
            dma((chan_count,)),
        ],
        compiler_params=pltpu.CompilerParams(
            collective_id=0, has_side_effects=True, vmem_limit_bytes=48 * 2**20
        ),
    )(tokens, jnp.swapaxes(w_in, 0, 1), order)


def output_kernel(
    seq_count, chan_count, folded, w, out,
    landed, wbuf, kept, inner_out, inner_in, across_out, across_in,
    row_send, row_recv, inner_send, inner_recv, across_send, across_recv, w_sem,
):
    seq, chip, core, chips = place(seq_count, chan_count)
    rows_to, across, sibling = partners(seq, chip, core, seq_count, chips)
    f32 = jnp.float32
    width = out.shape[1]
    tile = min(512, width)
    load = pltpu.make_async_copy(w, wbuf, w_sem)
    load.start()
    greet(rows_to + across + [sibling])
    row_sems = (row_send, row_recv)
    copies = {h: exchange_rows(folded, landed, row_sems, seq, rows_to, h) for h in HALVES}

    half_rows = landed.shape[1]

    def multiply(halves, c, target, slot):
        @pl.loop(0, width // tile)
        def _(t):
            start = pl.multiple_of(t * tile, tile)
            cols = pl.ds(pl.multiple_of(c * width + start, tile), tile)
            lhs = jnp.concatenate([landed[h] for h in halves])
            term = jnp.dot(lhs, wbuf[:, cols], preferred_element_type=f32).astype(target.dtype)
            for n, h in enumerate(halves):
                rows = term[n * half_rows : (n + 1) * half_rows]
                target[h, slot, :, pl.ds(start, tile)] = rows

    inners, outs = {0: [], 1: []}, {0: [], 1: []}

    def share(halves, c, slot):
        multiply(halves, c * 2 + 1 - core, inner_out, slot)
        for h in halves:
            src, dst = inner_out.at[h, slot], inner_in.at[h, slot]
            index = h * chips + slot
            inners[h].append(remote(src, dst, (inner_send, inner_recv), index, sibling))
            inners[h][-1].start()
        multiply(halves, c * 2 + core, kept, slot)

    for h in HALVES:
        for copy in copies[h]:
            copy.wait()
        if h == HALVES[0]:
            load.wait()
        for o in range(1, chips):
            n = o - 1
            share((h,), lax.rem(chip + o, chips), n)
            inners[h][-1].wait_recv()
            across_out[h, n] = (kept[h, n] + inner_in[h, n].astype(f32)).astype(jnp.bfloat16)
            src, dst = across_out.at[h, n], across_in.at[h, n]
            index = h * (chips - 1) + n
            outs[h].append(remote(src, dst, (across_send, across_recv), index, across[n]))
            outs[h][-1].start()
    share(HALVES, chip, chips - 1)

    part = landed.shape[1] // seq_count
    for h in HALVES:
        inners[h][-1].wait_recv()
        result = kept[h, chips - 1] + inner_in[h, chips - 1].astype(f32)
        for o in range(1, chips):
            outs[h][o - 1].wait_recv()
            result = result + across_in[h, o - 1].astype(f32)
        result = result.astype(out.dtype)
        for d in range(seq_count):
            out[pl.ds((2 * d + h) * part, part)] = result[d * part : (d + 1) * part]
    for h in HALVES:
        for copy in inners[h] + outs[h]:
            copy.wait_send()


def project_out(folded, w_out, seq_count, chan_count):
    rows, chans = folded.shape
    width = w_out.shape[1] // chan_count
    chips = chan_count // 2
    vmem = pl.BlockSpec(memory_space=pltpu.VMEM)
    bf16 = jnp.bfloat16
    dma = pltpu.SemaphoreType.DMA
    slots = lambda count: pltpu.VMEM((2, count, rows // 2, width), bf16)
    return pl.pallas_call(
        functools.partial(output_kernel, seq_count, chan_count),
        out_shape=jax.ShapeDtypeStruct((rows, width), bf16),
        in_specs=[vmem, pl.BlockSpec(memory_space=pl.ANY)],
        out_specs=vmem,
        scratch_shapes=[
            pltpu.VMEM((2, rows // 2, chans), bf16),
            pltpu.VMEM(w_out.shape, bf16),
            pltpu.VMEM((2, chips, rows // 2, width), jnp.float32),
            slots(chips),
            slots(chips),
            slots(chips - 1),
            slots(chips - 1),
            dma((2 * (seq_count - 1),)),
            dma((2 * (seq_count - 1),)),
            dma((2 * chips,)),
            dma((2 * chips,)),
            dma((2 * (chips - 1),)),
            dma((2 * (chips - 1),)),
            dma(()),
        ],
        compiler_params=pltpu.CompilerParams(
            collective_id=1, has_side_effects=True, vmem_limit_bytes=32 * 2**20
        ),
    )(folded, w_out)


def body(tokens, w_in, short_filter, mr_filter, skip_gain, w_out, segments):
    rows, width = tokens.shape
    seq_count = lax.axis_size("seq")
    taps = mr_filter.shape[1]
    fold = fold_matrix(rows, seq_count)
    chan_size = lax.axis_size("chan")
    if rows // seq_count % (2 * PACK) == 0 and chan_size % 2 == 0 and chan_size > 2:
        q, k, v, *halos = project(tokens, w_in, fold_matrix(rows // 2, seq_count).T, taps, seq_count, chan_size)
        folded = mix((q, k, v), halos, short_filter, mr_filter, skip_gain, segments, fold)
        return project_out(folded, w_out, seq_count, chan_size)
    pieces = tokens.reshape(seq_count, rows // seq_count, width)
    received = lax.all_to_all(pieces, "seq", split_axis=0, concat_axis=0, tiled=True)
    ordered = lax.dot_general(
        fold,
        received.reshape(rows, width),
        (((0,), (0,)), ((), ())),
        preferred_element_type=jnp.float32,
    ).astype(jnp.bfloat16)
    gathered = lax.all_gather(ordered, "chan", axis=1, tiled=True)
    q, k, v = [
        jnp.dot(gathered, w_in[:, i], preferred_element_type=jnp.float32).astype(jnp.bfloat16)
        for i in range(3)
    ]
    tails = (q[rows - PACK :], k[rows - taps - PACK :], v[rows - taps - PACK :])
    ring = [(i, i + 1) for i in range(seq_count - 1)]
    halos = lax.ppermute(tails, "seq", ring)
    folded = mix((q, k, v), halos, short_filter, mr_filter, skip_gain, segments, fold)
    outgoing = folded.reshape(seq_count, rows // seq_count, folded.shape[1])
    returned = lax.all_to_all(outgoing, "seq", split_axis=0, concat_axis=0, tiled=True)
    partial = jnp.dot(
        returned.reshape(rows, -1), w_out, preferred_element_type=jnp.float32
    ).astype(jnp.bfloat16)
    return lax.psum_scatter(partial, "chan", scatter_dimension=1, tiled=True)


def solution(mesh):
    return jax.shard_map(
        body,
        mesh=mesh,
        in_specs=(
            P("seq", "chan"),
            P(None, None, "chan"),
            P(None, None, "chan"),
            P("chan", None),
            P("chan"),
            P("chan", None),
            P(),
        ),
        out_specs=P("seq", "chan"),
        check_vma=False,
    )
```
